128 devices in a mesh: replica: 4 (over z), fsdp: 32 (over y, x, core).
Axes of the slice: x: 4, y: 4, z: 4, core: 2. Of those that a mesh axis runs over, the one named last changes fastest.
Arguments:
- tokens: bfloat16 [4, 16384, 8192], P('replica', 'fsdp'), may hold values from -6 to 6
- next_weights: bfloat16 [4, 8192, 2048], P('replica', 'fsdp'), may hold values from -0.0625 to 0.0625
- inner_weights: bfloat16 [4, 2, 8192, 2048], P('replica', None, 'fsdp'), as said below
- global_weights: float32 [2, 8192, 2048], P(None, 'fsdp', 'replica'), as said below
- momentum: float32 [2, 8192, 2048], P(None, 'fsdp', 'replica'), may hold values from -2 to 2
Outputs:
- projected: bfloat16 [4, 16384, 2048], P('replica', 'fsdp')
- new_global: float32 [2, 8192, 2048], P(None, 'fsdp', 'replica')
- new_momentum: float32 [2, 8192, 2048], P(None, 'fsdp', 'replica')
- normalized: bfloat16 [2, 8192, 2048], P(None, 'fsdp', 'replica')
- mixed_inner: bfloat16 [4, 2, 8192, 2048], P('replica', None, 'fsdp')
- amax: float32 [2, 2], replicated
The draws below stay inside these ranges and needn't reach their ends.
Inputs may be any that keep to these rules, and one draw needn't show every extreme that they name: `inner_weights`: entries of order a tenth; each replica's inner weights differ from the outer copy by a drift of a fraction of the entry's scale. `global_weights`: entries of order a tenth.
All inputs are finite; a program needn't handle non-finite values.
Results may differ from the reference program's by a relative error of at most 0.015.
Values may be sent and summed in bfloat16 or wider, within the bound.
A program may use at most 128 MiB of HBM per device.

```python
import math
import jax
import jax.numpy as jnp
from jax import lax

D = 8192
KVW = 1024
LAYERS = 2
TOKENS = 16384
REPLICAS = 4


def shared_base(key):
    keys = jax.random.split(key, 4)
    shape = (LAYERS, D, 2 * KVW)
    normal_vals = jax.random.normal(keys[0], shape, jnp.float32)
    row_factor = jnp.power(10.0, jnp.arange(D, dtype=jnp.float32) / D - 1.0)[None, :, None]
    col_factor = jnp.exp(jax.random.uniform(keys[2], (LAYERS, 1, 2 * KVW), jnp.float32) * math.log(10.0))
    rough = jnp.exp(jax.random.uniform(keys[3], shape, jnp.float32, -math.log(2.0), 0.0))
    scale = 0.05 * row_factor * col_factor * rough
    return (scale * normal_vals, scale)


def draw_global_weights(key, part):
    base, scale = shared_base(key)
    return base.astype(jnp.float32)


def draw_inner_weights(key, part):
    base, scale = shared_base(key)
    key = jax.random.fold_in(key, 7)
    drift = jax.random.normal(key, (REPLICAS, LAYERS, D, 2 * KVW), jnp.float32)
    return (base[None] + 0.3 * scale[None] * drift).astype(jnp.bfloat16)


def block_levels(rng, shape, shards, least, largest):
    gain = 1.0
    for dim, shards_of in shards:
        draws = jax.random.uniform(jax.random.fold_in(jax.random.fold_in(rng, 6), dim), (shards_of,), jnp.float32, least / len(shards), largest / len(shards))
        gain = gain * jnp.repeat(jnp.exp(draws), shape[dim] // shards_of).reshape((-1,) + (1,) * (len(shape) - 1 - dim))
    return gain


def noise(stream_key, shape, deviation, limit, cuts=(), held_as=jnp.bfloat16):
    result = jax.random.normal(stream_key, shape, jnp.float32) * deviation
    if len(cuts) > 0:
        result = block_levels(stream_key, shape, cuts, -0.22, 0.18) * result
    return jnp.clip(result, min=-limit, max=limit).astype(held_as)


def setup_inputs(seed: int = 0) -> dict:
    splits = jax.random.split(jax.random.key(seed), 6)
    return {
        "tokens": noise(splits[0], (REPLICAS, TOKENS, D), 1.0, 6.0, ((0, 4), (1, 32))),
        "next_weights": noise(splits[1], (REPLICAS, D, 2 * KVW), D ** -0.5, 0.0625, ((0, 4), (1, 32))),
        "inner_weights": draw_inner_weights(jax.random.fold_in(splits[5], 71), 0),
        "global_weights": draw_global_weights(jax.random.fold_in(splits[5], 71), 0),
        "momentum": noise(splits[4], (LAYERS, D, 2 * KVW), 0.3, 2.0, ((1, 32), (2, 4)), jnp.float32),
    }


outer_rate = 0.7
outer_mom = 0.9
mix_share = 0.5


def project_pair(pair):
    return jnp.dot(pair[0], pair[1], preferred_element_type=jnp.float32).astype(jnp.bfloat16)


def reference(tokens, next_weights, inner_weights, global_weights, momentum):
    projected = lax.map(project_pair, (tokens, next_weights))
    inner_sum = jnp.sum(inner_weights.astype(jnp.float32), axis=0)
    pseudo = global_weights - inner_sum / REPLICAS
    new_momentum = outer_mom * momentum + pseudo
    new_global = global_weights - outer_rate * (pseudo + outer_mom * new_momentum)
    magnitude = jnp.abs(new_global)
    amax = jnp.stack([jnp.max(magnitude[:, :, :KVW], axis=(1, 2)), jnp.max(magnitude[:, :, KVW:], axis=(1, 2))], axis=1)
    key_cols = (jnp.arange(2 * KVW) < KVW)[None, None, :]
    per_column = jnp.where(key_cols, amax[:, 0][:, None, None], amax[:, 1][:, None, None])
    normalized = (new_global / (per_column + 1e-6)).astype(jnp.bfloat16)
    rounded_global = lax.optimization_barrier(new_global.astype(jnp.bfloat16))
    mixed_inner = (mix_share * inner_weights.astype(jnp.float32) + (1.0 - mix_share) * rounded_global.astype(jnp.float32)[None]).astype(jnp.bfloat16)
    return projected, new_global, new_momentum, normalized, mixed_inner, amax
```

```python
import functools

import jax
import jax.numpy as jnp
from jax import lax
from jax.experimental import pallas as pl
from jax.experimental.pallas import tpu as pltpu
from jax.sharding import PartitionSpec as P

MESH = pl.DeviceIdType.MESH
KVW = 1024
SIDE = 4
REPLICAS = 4
DEPTH = 256
QUART = 256
ROWS = 512
COLS = 512
STEPS = 15
CHUNK = 512
outer_rate = 0.7
outer_mom = 0.9
mix_share = 0.5


def build_queues():
    def place(axis, along, across):
        return (along, across) if axis == 0 else (across, along)

    queues = {}
    for axis in (0, 1):
        first = (0, 1) if axis == 0 else (2, 3)
        late = (2, 3) if axis == 0 else (0, 1)
        for sign in (1, -1):
            via, other = (first, late) if sign == 1 else (first[::-1], late[::-1])
            items = [(via[0], 0, 0), (via[1], 0, 0), (via[0],) + place(axis, -sign, 0)]
            items += [(other[0], 0, 0), (other[1], 0, 0)]
            for quarter in other:
                items += [(quarter,) + place(axis, 0, across) for across in (-1, 1, 2)]
            items += [(other[0],) + place(axis, -sign, across) for across in (0, -1, 1, 2)]
            queues[axis, sign] = items
    return queues


QUEUES = build_queues()
WAYS = ((0, 1), (0, -1), (1, 1), (1, -1))


def arrivals(step):
    found = []
    for axis, sign in WAYS:
        quarter, ox, oy = QUEUES[axis, sign][step]
        found.append((quarter, ox - sign, oy) if axis == 0 else (quarter, ox, oy - sign))
    return [(quarter, ox % SIDE, oy % SIDE) for quarter, ox, oy in found]


def token_order():
    order = [(0, 0)]
    for step in range(STEPS):
        for _, ox, oy in arrivals(step):
            if (ox, oy) not in order:
                order.append((ox, oy))
    return order


ORDER = token_order()


def kernel(
    tokens,
    weights,
    inner,
    outer_in,
    momentum_in,
    projected,
    new_global,
    new_momentum,
    normalized,
    mixed,
    amax_out,
    tok,
    wts,
    acc,
    out_stage,
    inner_v,
    parts,
    outer_v,
    momentum_v,
    full,
    peaks,
    ring_send,
    ring_recv,
    tok_here,
    tok_send,
    tok_recv,
    wts_here,
    wts_send,
    wts_recv,
    sum_send,
    sum_recv,
    full_send,
    full_recv,
    peak_send,
    peak_recv,
    out_send,
    out_recv,
    local_sem,
):
    rep = lax.axis_index("replica")
    fsdp = lax.axis_index("fsdp")
    core = fsdp % 2
    x = (fsdp // 2) % SIDE
    y = fsdp // (2 * SIDE)

    def chip_at(ox, oy):
        return ((y + oy) % SIDE) * SIDE + (x + ox) % SIDE

    def at_plane(ox, oy):
        return {"replica": rep, "fsdp": chip_at(ox, oy) * 2 + core}

    def at_replica(oz):
        return {"replica": (rep + oz) % REPLICAS, "fsdp": fsdp}

    sibling = {"replica": rep, "fsdp": chip_at(0, 0) * 2 + 1 - core}
    me = chip_at(0, 0)

    def remote(src, dst, send, recv, device):
        return pltpu.make_async_remote_copy(
            src_ref=src, dst_ref=dst, send_sem=send, recv_sem=recv, device_id=device, device_id_type=MESH
        )

    my_rows = pl.ds(pl.multiple_of(core * ROWS, ROWS), ROWS)
    my_depth = pl.ds(pl.multiple_of(core * DEPTH, DEPTH), DEPTH)

    def columns(which, quarter):
        return pl.ds(pl.multiple_of(which * KVW + quarter * QUART, QUART), QUART)

    locals_ = []

    def start_local(src, dst, sem):
        copy = pltpu.make_async_copy(src, dst, sem)
        copy.start()
        return copy

    w_here = [
        start_local(weights.at[0, :, columns(core, q)], wts.at[me, q, my_depth, :], wts_here.at[q]) for q in range(4)
    ]

    barrier = pltpu.get_barrier_semaphore()
    peers = [sibling] + [at_plane(o, 0) for o in (1, 2, 3)] + [at_plane(0, o) for o in (1, 2, 3)]
    peers += [at_replica(o) for o in (1, 2, 3)]
    for peer in peers:
        pl.semaphore_signal(barrier, inc=1, device_id=peer, device_id_type=MESH)
    pl.semaphore_wait(barrier, len(peers))

    w_far = []
    for q in range(4):
        copy = remote(
            weights.at[0, :, columns(1 - core, q)], wts.at[me, q, my_depth, :], wts_send.at[q], wts_recv.at[q], sibling
        )
        copy.start()
        w_far.append(copy)

    sums = []
    for oz in (1, 2, 3):
        target = (rep + oz) % REPLICAS
        copy = remote(
            inner.at[0, :, :, pl.ds(pl.multiple_of(target * COLS, COLS), COLS)],
            parts.at[rep],
            sum_send.at[oz - 1],
            sum_recv.at[oz - 1],
            at_replica(oz),
        )
        copy.start()
        sums.append(copy)

    def ring_copy(way, step):
        axis, sign = WAYS[way]
        quarter, ox, oy = QUEUES[axis, sign][step]
        block = wts.at[chip_at(ox, oy), quarter]
        device = at_plane(sign, 0) if axis == 0 else at_plane(0, sign)
        return remote(block, block, ring_send.at[way, step], ring_recv.at[way, step], device)

    for q in range(4):
        w_here[q].wait()
        w_far[q].wait_recv()
    ring = {}
    for step in (0, 1):
        for way in range(4):
            ring[way, step] = ring_copy(way, step)
            ring[way, step].start()

    tok_copies = {}
    for n, (ox, oy) in enumerate(ORDER):
        chip = chip_at(ox, oy)
        src = tokens.at[0, :, pl.ds(pl.multiple_of(chip * 2 * DEPTH, 2 * DEPTH), 2 * DEPTH)]
        dst = tok.at[chip, my_rows, :]
        here = start_local(src, dst, tok_here.at[n])
        far = remote(src, dst, tok_send.at[n], tok_recv.at[n], sibling)
        far.start()
        tok_copies[ox, oy] = (here, far)

    own_cols = pl.ds(pl.multiple_of(rep * COLS, COLS), COLS)
    outer_copies = [
        start_local(outer_in, outer_v, local_sem.at[0]),
        start_local(momentum_in, momentum_v, local_sem.at[1]),
        start_local(inner.at[0, :, :, own_cols], parts.at[rep], local_sem.at[2]),
        start_local(inner.at[0], inner_v, local_sem.at[3]),
    ]

    have = set()

    def need_tokens(spots):
        for spot in spots:
            if spot not in have:
                have.add(spot)
                here, far = tok_copies[spot]
                here.wait()
                far.wait_recv()

    def pick(i, values):
        result = values[0]
        for n in range(1, len(values)):
            result = jnp.where(i == n, values[n], result)
        return result

    chunks = 2 * ROWS // CHUNK

    def multiply(items, first):
        need_tokens([(ox, oy) for _, ox, oy in items])
        chips = [chip_at(ox, oy) for _, ox, oy in items]
        quarters = [q for q, _, _ in items]

        def body(i, carry):
            n, m = i // chunks, i % chunks
            chip, quarter = pick(n, chips), pick(n, quarters)
            rows = pl.ds(pl.multiple_of(m * CHUNK, CHUNK), CHUNK)
            part = jnp.dot(tok[chip, rows, :], wts[chip, quarter], preferred_element_type=jnp.float32)
            if first:
                acc[quarter, rows, :] = part
            else:
                acc[quarter, rows, :] += part
            return carry

        lax.fori_loop(0, len(items) * chunks, body, 0)

    LINES = 32
    is_value = rep // 2

    def update():
        for copy in outer_copies[:3]:
            copy.wait()
        for copy in sums:
            copy.wait_recv()
        highest = []
        for layer in range(2):

            def body(i, carry, layer=layer):
                rows = pl.ds(pl.multiple_of(i * LINES, LINES), LINES)
                total = parts[0, layer, rows, :].astype(jnp.float32)
                for r in range(1, REPLICAS):
                    total += parts[r, layer, rows, :].astype(jnp.float32)
                outer = outer_v[layer, rows, :]
                pseudo = outer - total / REPLICAS
                moved = outer_mom * momentum_v[layer, rows, :] + pseudo
                stepped = outer - outer_rate * (pseudo + outer_mom * moved)
                new_momentum[layer, rows, :] = moved
                new_global[layer, rows, :] = stepped
                full[rep, layer, rows, :] = stepped.astype(jnp.bfloat16)
                return jnp.maximum(carry, jnp.abs(stepped))

            top = lax.fori_loop(0, DEPTH // LINES, body, jnp.zeros((LINES, COLS), jnp.float32))
            highest.append(jnp.max(jnp.max(top, axis=0, keepdims=True), axis=1, keepdims=True))
        line = lax.broadcasted_iota(jnp.int32, (8, 128), 0)
        tile = jnp.where(
            line == is_value, highest[0], jnp.where(line == 2 + is_value, highest[1], jnp.zeros((8, 128), jnp.float32))
        )
        copies = []
        for oz in (1, 2, 3):
            copy = remote(
                full.at[rep], full.at[rep], full_send.at[oz - 1], full_recv.at[oz - 1], at_replica(oz)
            )
            copy.start()
            copies.append(copy)
        return tile, copies

    def send_peaks(stage, tile):
        peaks[stage, 0] = tile
        if stage == 3:
            devices = [sibling]
        else:
            devices = [(at_replica(o), at_plane(0, o), at_plane(o, 0))[stage] for o in (1, 2, 3)]
        copies = []
        for n, device in enumerate(devices):
            copy = remote(
                peaks.at[stage, 0], peaks.at[stage, n + 1], peak_send.at[stage, n], peak_recv.at[stage, n], device
            )
            copy.start()
            copies.append(copy)
        return copies

    def take_peaks(stage, copies):
        for copy in copies:
            copy.wait_recv()
        tile = peaks[stage, 0]
        for n in range(len(copies)):
            tile = jnp.maximum(tile, peaks[stage, n + 1])
        return tile

    def normalize(tile):
        values = [[tile[2 * l + t : 2 * l + t + 1, 0:1] for t in range(2)] for l in range(2)]
        row = lax.broadcasted_iota(jnp.int32, (2, 2), 0)
        col = lax.broadcasted_iota(jnp.int32, (2, 2), 1)
        amax_out[...] = jnp.where(
            row == 0,
            jnp.where(col == 0, values[0][0], values[0][1]),
            jnp.where(col == 0, values[1][0], values[1][1]),
        )
        for layer in range(2):
            scale = jnp.where(is_value == 0, values[layer][0], values[layer][1]) + 1e-06

            def body(i, carry, layer=layer, scale=scale):
                rows = pl.ds(pl.multiple_of(i * LINES, LINES), LINES)
                normalized[layer, rows, :] = (new_global[layer, rows, :] / scale).astype(jnp.bfloat16)
                return carry

            lax.fori_loop(0, DEPTH // LINES, body, 0)

    def mix(copies):
        outer_copies[3].wait()
        for copy in copies:
            copy.wait_recv()

        def body(i, carry):
            layer, n = i // (DEPTH // LINES), i % (DEPTH // LINES)
            rows = pl.ds(pl.multiple_of(n * LINES, LINES), LINES)
            for r in range(REPLICAS):
                cols = slice(r * COLS, (r + 1) * COLS)
                value = mix_share * inner_v[layer, rows, cols].astype(jnp.float32)
                value += (1.0 - mix_share) * full[r, layer, rows, :].astype(jnp.float32)
                mixed[0, layer, rows, cols] = value.astype(jnp.bfloat16)
            return carry

        lax.fori_loop(0, 2 * DEPTH // LINES, body, 0)

    multiply([(q, 0, 0) for q in range(4)], True)
    peak_copies = {}
    full_copies = None
    for step in range(STEPS):
        for way in range(4):
            ring[way, step].wait_recv()
        for way in range(4):
            if step + 2 < STEPS:
                ring[way, step].wait_send()
                ring[way, step + 2] = ring_copy(way, step + 2)
                ring[way, step + 2].start()
        if step < STEPS - 1:
            multiply(arrivals(step), False)
        if step == 5:
            tile, full_copies = update()
            peak_copies[0] = send_peaks(0, tile)
        if step in (6, 7, 8):
            tile = take_peaks(step - 6, peak_copies[step - 6])
            peak_copies[step - 5] = send_peaks(step - 5, tile)
        if step == 9:
            tile = take_peaks(3, peak_copies[3])
            normalize(tile)
        if step == 11:
            mix(full_copies)

    last = arrivals(STEPS - 1)
    need_tokens([(ox, oy) for _, ox, oy in last])
    out_copies = []
    other_rows = pl.ds(pl.multiple_of((1 - core) * ROWS, ROWS), ROWS)
    for q, ox, oy in last:
        chip = chip_at(ox, oy)
        part = jnp.dot(tok[chip, other_rows, :], wts[chip, q], preferred_element_type=jnp.float32)
        out_stage[q] = (acc[q, other_rows, :] + part).astype(jnp.bfloat16)
        copy = remote(out_stage.at[q], projected.at[0, :, columns(core, q)], out_send.at[q], out_recv.at[q], sibling)
        copy.start()
        out_copies.append(copy)
    for q, ox, oy in last:
        chip = chip_at(ox, oy)
        part = jnp.dot(tok[chip, my_rows, :], wts[chip, q], preferred_element_type=jnp.float32)
        projected[0, :, columns(core, q)] = (acc[q, my_rows, :] + part).astype(jnp.bfloat16)

    for way in range(4):
        for step in (STEPS - 2, STEPS - 1):
            ring[way, step].wait_send()
    for copy in w_far + sums + full_copies + [far for _, far in tok_copies.values()]:
        copy.wait_send()
    for copies in peak_copies.values():
        for copy in copies:
            copy.wait_send()
    for copy in out_copies:
        copy.wait()


def on_device(tokens, next_weights, inner_weights, global_weights, momentum):
    bf16, f32 = jnp.bfloat16, jnp.float32
    dma = pltpu.SemaphoreType.DMA
    any_ = pl.BlockSpec(memory_space=pl.ANY)
    vmem = pl.BlockSpec(memory_space=pltpu.VMEM)
    layers, depth, wide = inner_weights.shape[1:]
    return pl.pallas_call(
        kernel,
        name="project_and_outer_step",
        out_shape=(
            jax.ShapeDtypeStruct((1, ROWS, 2 * KVW), bf16),
            jax.ShapeDtypeStruct((layers, depth, COLS), f32),
            jax.ShapeDtypeStruct((layers, depth, COLS), f32),
            jax.ShapeDtypeStruct((layers, depth, COLS), bf16),
            jax.ShapeDtypeStruct((1, layers, depth, wide), bf16),
            jax.ShapeDtypeStruct((2, 2), f32),
        ),
        in_specs=[any_] * 5,
        out_specs=(vmem,) * 6,
        scratch_shapes=[
            pltpu.VMEM((SIDE * SIDE, 2 * ROWS, 2 * DEPTH), bf16),
            pltpu.VMEM((SIDE * SIDE, 4, 2 * DEPTH, QUART), bf16),
            pltpu.VMEM((4, 2 * ROWS, QUART), f32),
            pltpu.VMEM((4, ROWS, QUART), bf16),
            pltpu.VMEM((layers, depth, wide), bf16),
            pltpu.VMEM((REPLICAS, layers, depth, COLS), bf16),
            pltpu.VMEM((layers, depth, COLS), f32),
            pltpu.VMEM((layers, depth, COLS), f32),
            pltpu.VMEM((REPLICAS, layers, depth, COLS), bf16),
            pltpu.VMEM((4, 4, 8, 128), f32),
            dma((4, STEPS)),
            dma((4, STEPS)),
            dma((16,)),
            dma((16,)),
            dma((16,)),
            dma((4,)),
            dma((4,)),
            dma((4,)),
            dma((3,)),
            dma((3,)),
            dma((3,)),
            dma((3,)),
            dma((4, 3)),
            dma((4, 3)),
            dma((4,)),
            dma((4,)),
            dma((4,)),
        ],
        compiler_params=pltpu.CompilerParams(
            collective_id=0, has_side_effects=True, vmem_limit_bytes=56 * 1024 * 1024
        ),
    )(tokens, next_weights, inner_weights, global_weights, momentum)


def solution(mesh):
    placed = (
        P("replica", "fsdp", None),
        P("replica", "fsdp", None),
        P("replica", None, "fsdp", None),
        P(None, "fsdp", "replica"),
        P(None, "fsdp", "replica"),
    )
    return jax.shard_map(
        on_device,
        mesh=mesh,
        in_specs=placed,
        out_specs=(
            P("replica", "fsdp", None),
            P(None, "fsdp", "replica"),
            P(None, "fsdp", "replica"),
            P(None, "fsdp", "replica"),
            P("replica", None, "fsdp", None),
            P(),
        ),
        check_vma=False,
    )
```

```python
import functools

import jax
import jax.numpy as jnp
from jax import lax
from jax.experimental import pallas as pl
from jax.experimental.pallas import tpu as pltpu
from jax.sharding import PartitionSpec as P

MESH = pl.DeviceIdType.MESH
KVW = 1024
SIDE = 4
REPLICAS = 4
DEPTH = 256
QUART = 256
ROWS = 512
COLS = 512
STEPS = 15
AHEAD = 3
CHUNK = 512
outer_rate = 0.7
outer_mom = 0.9
mix_share = 0.5


def build_queues():
    def place(axis, along, across):
        return (along, across) if axis == 0 else (across, along)

    queues = {}
    for axis in (0, 1):
        first = (0, 1) if axis == 0 else (2, 3)
        late = (2, 3) if axis == 0 else (0, 1)
        for sign in (1, -1):
            via, other = (first, late) if sign == 1 else (first[::-1], late[::-1])
            items = [(via[0], 0, 0), (via[1], 0, 0), (other[0], 0, 0), (other[1], 0, 0)]
            items += [(via[0],) + place(axis, -sign, 0)]
            items += [(quarter,) + place(axis, 0, across) for quarter in other for across in (-1, 1)]
            items += [(quarter,) + place(axis, 0, 2) for quarter in other]
            items += [(other[0],) + place(axis, -sign, across) for across in (0, -1, 1, 2)]
            queues[axis, sign] = items
    return queues


QUEUES = build_queues()
WAYS = ((0, 1), (0, -1), (1, 1), (1, -1))


def arrivals(step):
    found = []
    for axis, sign in WAYS:
        quarter, ox, oy = QUEUES[axis, sign][step]
        found.append((quarter, ox - sign, oy) if axis == 0 else (quarter, ox, oy - sign))
    return [(quarter, ox % SIDE, oy % SIDE) for quarter, ox, oy in found]


def token_order():
    order = [(0, 0)]
    for step in range(STEPS):
        for _, ox, oy in arrivals(step):
            if (ox, oy) not in order:
                order.append((ox, oy))
    return order


ORDER = token_order()


def kernel(
    tokens,
    weights,
    inner,
    outer_in,
    momentum_in,
    projected,
    new_global,
    new_momentum,
    normalized,
    mixed,
    amax_out,
    tok,
    wts,
    acc,
    out_stage,
    inner_v,
    parts,
    outer_v,
    momentum_v,
    full,
    peaks,
    ring_send,
    ring_recv,
    tok_here,
    tok_send,
    tok_recv,
    wts_here,
    wts_send,
    wts_recv,
    sum_send,
    sum_recv,
    full_send,
    full_recv,
    peak_send,
    peak_recv,
    out_send,
    out_recv,
    local_sem,
):
    rep = lax.axis_index("replica")
    fsdp = lax.axis_index("fsdp")
    core = fsdp % 2
    x = (fsdp // 2) % SIDE
    y = fsdp // (2 * SIDE)

    def chip_at(ox, oy):
        return ((y + oy) % SIDE) * SIDE + (x + ox) % SIDE

    def at_plane(ox, oy):
        return {"replica": rep, "fsdp": chip_at(ox, oy) * 2 + core}

    def at_replica(oz):
        return {"replica": (rep + oz) % REPLICAS, "fsdp": fsdp}

    sibling = {"replica": rep, "fsdp": chip_at(0, 0) * 2 + 1 - core}
    me = chip_at(0, 0)

    def remote(src, dst, send, recv, device):
        return pltpu.make_async_remote_copy(
            src_ref=src, dst_ref=dst, send_sem=send, recv_sem=recv, device_id=device, device_id_type=MESH
        )

    my_rows = pl.ds(pl.multiple_of(core * ROWS, ROWS), ROWS)
    my_depth = pl.ds(pl.multiple_of(core * DEPTH, DEPTH), DEPTH)

    def columns(which, quarter):
        return pl.ds(pl.multiple_of(which * KVW + quarter * QUART, QUART), QUART)

    def start_local(src, dst, sem):
        copy = pltpu.make_async_copy(src, dst, sem)
        copy.start()
        return copy

    w_here = [
        start_local(weights.at[0, :, columns(core, q)], wts.at[me, q, my_depth, :], wts_here.at[q]) for q in range(4)
    ]

    barrier = pltpu.get_barrier_semaphore()
    peers = [sibling] + [at_plane(o, 0) for o in (1, 2, 3)] + [at_plane(0, o) for o in (1, 2, 3)]
    peers += [at_replica(o) for o in (1, 2, 3)]
    for peer in peers:
        pl.semaphore_signal(barrier, inc=1, device_id=peer, device_id_type=MESH)
    pl.semaphore_wait(barrier, len(peers))

    w_far = []
    for q in range(4):
        copy = remote(
            weights.at[0, :, columns(1 - core, q)], wts.at[me, q, my_depth, :], wts_send.at[q], wts_recv.at[q], sibling
        )
        copy.start()
        w_far.append(copy)

    def ring_copy(way, step):
        axis, sign = WAYS[way]
        quarter, ox, oy = QUEUES[axis, sign][step]
        device = at_plane(sign, 0) if axis == 0 else at_plane(0, sign)
        block = wts.at[chip_at(ox, oy), quarter]
        if step > 1:
            return [remote(block, block, ring_send.at[way, step], ring_recv.at[way, step], device)]
        copies = []
        for half, which in enumerate((core, 1 - core)):
            part = wts.at[me, quarter, pl.ds(pl.multiple_of(which * DEPTH, DEPTH), DEPTH), :]
            slot = step if half == 0 else STEPS + step
            copies.append(remote(part, part, ring_send.at[way, slot], ring_recv.at[way, slot], device))
        return copies

    ring = {(way, step): ring_copy(way, step) for way in range(4) for step in range(AHEAD)}
    for copy in w_here:
        copy.wait()
    for step in (0, 1):
        for way in range(4):
            ring[way, step][0].start()

    sums = []
    for oz in (1, 2, 3):
        target = (rep + oz) % REPLICAS
        copy = remote(
            inner.at[0, :, :, pl.ds(pl.multiple_of(target * COLS, COLS), COLS)],
            parts.at[rep],
            sum_send.at[oz - 1],
            sum_recv.at[oz - 1],
            at_replica(oz),
        )
        copy.start()
        sums.append(copy)

    for copy in w_far:
        copy.wait_recv()
    for step in range(AHEAD):
        for way in range(4):
            ring[way, step][-1].start()

    tok_copies = {}
    for n, (ox, oy) in enumerate(ORDER):
        chip = chip_at(ox, oy)
        src = tokens.at[0, :, pl.ds(pl.multiple_of(chip * 2 * DEPTH, 2 * DEPTH), 2 * DEPTH)]
        dst = tok.at[chip, my_rows, :]
        here = start_local(src, dst, tok_here.at[n])
        far = remote(src, dst, tok_send.at[n], tok_recv.at[n], sibling)
        far.start()
        tok_copies[ox, oy] = (here, far)

    own_cols = pl.ds(pl.multiple_of(rep * COLS, COLS), COLS)
    outer_copies = [
        start_local(outer_in, outer_v, local_sem.at[0]),
        start_local(momentum_in, momentum_v, local_sem.at[1]),
        start_local(inner.at[0, :, :, own_cols], parts.at[rep], local_sem.at[2]),
        start_local(inner.at[0], inner_v, local_sem.at[3]),
    ]

    have = set()

    def need_tokens(spots):
        for spot in spots:
            if spot not in have:
                have.add(spot)
                here, far = tok_copies[spot]
                here.wait()
                far.wait_recv()

    def pick(i, values):
        result = values[0]
        for n in range(1, len(values)):
            result = jnp.where(i == n, values[n], result)
        return result

    chunks = 2 * ROWS // CHUNK

    def multiply(items, first):
        need_tokens([(ox, oy) for _, ox, oy in items])
        chips = [chip_at(ox, oy) for _, ox, oy in items]
        quarters = [q for q, _, _ in items]

        def body(i, carry):
            n, m = i // chunks, i % chunks
            chip, quarter = pick(n, chips), pick(n, quarters)
            rows = pl.ds(pl.multiple_of(m * CHUNK, CHUNK), CHUNK)
            part = jnp.dot(tok[chip, rows, :], wts[chip, quarter], preferred_element_type=jnp.float32)
            if first:
                acc[quarter, rows, :] = part
            else:
                acc[quarter, rows, :] += part
            return carry

        lax.fori_loop(0, len(items) * chunks, body, 0)

    LINES = 32
    is_value = rep // 2

    def update():
        for copy in outer_copies[:3]:
            copy.wait()
        for copy in sums:
            copy.wait_recv()
        highest = []
        for layer in range(2):

            def body(i, carry, layer=layer):
                rows = pl.ds(pl.multiple_of(i * LINES, LINES), LINES)
                total = parts[0, layer, rows, :].astype(jnp.float32)
                for r in range(1, REPLICAS):
                    total += parts[r, layer, rows, :].astype(jnp.float32)
                outer = outer_v[layer, rows, :]
                pseudo = outer - total / REPLICAS
                moved = outer_mom * momentum_v[layer, rows, :] + pseudo
                stepped = outer - outer_rate * (pseudo + outer_mom * moved)
                new_momentum[layer, rows, :] = moved
                new_global[layer, rows, :] = stepped
                full[rep, layer, rows, :] = stepped.astype(jnp.bfloat16)
                return jnp.maximum(carry, jnp.abs(stepped))

            top = lax.fori_loop(0, DEPTH // LINES, body, jnp.zeros((LINES, COLS), jnp.float32))
            highest.append(jnp.max(jnp.max(top, axis=0, keepdims=True), axis=1, keepdims=True))
        line = lax.broadcasted_iota(jnp.int32, (8, 128), 0)
        tile = jnp.where(
            line == is_value, highest[0], jnp.where(line == 2 + is_value, highest[1], jnp.zeros((8, 128), jnp.float32))
        )
        peak_copies[0] = send_peaks(0, tile)
        copies = []
        for oz in (1, 2, 3):
            copy = remote(
                full.at[rep], full.at[rep], full_send.at[oz - 1], full_recv.at[oz - 1], at_replica(oz)
            )
            copy.start()
            copies.append(copy)
        return copies

    def send_peaks(stage, tile):
        peaks[stage, 0] = tile
        if stage == 3:
            devices = [sibling]
        else:
            devices = [(at_replica(o), at_plane(0, o), at_plane(o, 0))[stage] for o in (1, 2, 3)]
        copies = []
        for n, device in enumerate(devices):
            copy = remote(
                peaks.at[stage, 0], peaks.at[stage, n + 1], peak_send.at[stage, n], peak_recv.at[stage, n], device
            )
            copy.start()
            copies.append(copy)
        return copies

    def take_peaks(stage, copies):
        for copy in copies:
            copy.wait_recv()
        tile = peaks[stage, 0]
        for n in range(len(copies)):
            tile = jnp.maximum(tile, peaks[stage, n + 1])
        return tile

    def normalize(tile):
        values = [[tile[2 * l + t : 2 * l + t + 1, 0:1] for t in range(2)] for l in range(2)]
        row = lax.broadcasted_iota(jnp.int32, (2, 2), 0)
        col = lax.broadcasted_iota(jnp.int32, (2, 2), 1)
        amax_out[...] = jnp.where(
            row == 0,
            jnp.where(col == 0, values[0][0], values[0][1]),
            jnp.where(col == 0, values[1][0], values[1][1]),
        )
        for layer in range(2):
            scale = jnp.where(is_value == 0, values[layer][0], values[layer][1]) + 1e-06

            def body(i, carry, layer=layer, scale=scale):
                rows = pl.ds(pl.multiple_of(i * LINES, LINES), LINES)
                normalized[layer, rows, :] = (new_global[layer, rows, :] / scale).astype(jnp.bfloat16)
                return carry

            lax.fori_loop(0, DEPTH // LINES, body, 0)

    def mix(copies):
        outer_copies[3].wait()
        for copy in copies:
            copy.wait_recv()

        def body(i, carry):
            layer, n = i // (DEPTH // LINES), i % (DEPTH // LINES)
            rows = pl.ds(pl.multiple_of(n * LINES, LINES), LINES)
            for r in range(REPLICAS):
                cols = slice(r * COLS, (r + 1) * COLS)
                value = mix_share * inner_v[layer, rows, cols].astype(jnp.float32)
                value += (1.0 - mix_share) * full[r, layer, rows, :].astype(jnp.float32)
                mixed[0, layer, rows, cols] = value.astype(jnp.bfloat16)
            return carry

        lax.fori_loop(0, 2 * DEPTH // LINES, body, 0)

    multiply([(q, 0, 0) for q in range(4)], True)
    peak_copies = {}
    full_copies = []
    for step in range(STEPS):
        for way in range(4):
            for copy in ring[way, step]:
                copy.wait_recv()
        if step + AHEAD < STEPS:
            for way in range(4):
                for copy in ring[way, step]:
                    copy.wait_send()
                ring[way, step + AHEAD] = ring_copy(way, step + AHEAD)
                ring[way, step + AHEAD][0].start()
        if step < STEPS - 1:
            multiply(arrivals(step), False)
        if step == 4:
            full_copies = update()
        if step in (6, 8, 10):
            stage = step // 2 - 3
            tile = take_peaks(stage, peak_copies[stage])
            peak_copies[stage + 1] = send_peaks(stage + 1, tile)
        if step == 11:
            normalize(take_peaks(3, peak_copies[3]))
        if step == 12:
            mix(full_copies)

    last = arrivals(STEPS - 1)
    need_tokens([(ox, oy) for _, ox, oy in last])
    out_copies = []
    other_rows = pl.ds(pl.multiple_of((1 - core) * ROWS, ROWS), ROWS)
    for q, ox, oy in last:
        chip = chip_at(ox, oy)
        part = jnp.dot(tok[chip, other_rows, :], wts[chip, q], preferred_element_type=jnp.float32)
        out_stage[q] = (acc[q, other_rows, :] + part).astype(jnp.bfloat16)
        copy = remote(out_stage.at[q], projected.at[0, :, columns(core, q)], out_send.at[q], out_recv.at[q], sibling)
        copy.start()
        out_copies.append(copy)
    for q, ox, oy in last:
        chip = chip_at(ox, oy)
        part = jnp.dot(tok[chip, my_rows, :], wts[chip, q], preferred_element_type=jnp.float32)
        projected[0, :, columns(core, q)] = (acc[q, my_rows, :] + part).astype(jnp.bfloat16)

    for way in range(4):
        for step in range(STEPS - AHEAD, STEPS):
            ring[way, step][0].wait_send()
    for copy in w_far + sums + full_copies + [far for _, far in tok_copies.values()]:
        copy.wait_send()
    for copies in peak_copies.values():
        for copy in copies:
            copy.wait_send()
    for copy in out_copies:
        copy.wait()


def write_out(*refs):
    n = len(refs) // 2
    sem = refs[-1]
    copies = [pltpu.make_async_copy(refs[i], refs[n + i], sem.at[i]) for i in range(n)]
    for copy in copies:
        copy.start()
    for copy in copies:
        copy.wait()


def on_device(tokens, next_weights, inner_weights, global_weights, momentum):
    bf16, f32 = jnp.bfloat16, jnp.float32
    dma = pltpu.SemaphoreType.DMA
    any_ = pl.BlockSpec(memory_space=pl.ANY)
    vmem = pl.BlockSpec(memory_space=pltpu.VMEM)
    layers, depth, wide = inner_weights.shape[1:]
    results = (
        ((1, ROWS, 2 * KVW), bf16),
        ((layers, depth, COLS), f32),
        ((layers, depth, COLS), f32),
        ((layers, depth, COLS), bf16),
        ((1, layers, depth, wide), bf16),
        ((2, 2), f32),
    )
    held = pl.pallas_call(
        kernel,
        name="project_and_outer_step",
        out_shape=tuple(pltpu.VMEM(*result) for result in results),
        in_specs=[any_] * 5,
        out_specs=(vmem,) * 6,
        scratch_shapes=[
            pltpu.VMEM((SIDE * SIDE, 2 * ROWS, 2 * DEPTH), bf16),
            pltpu.VMEM((SIDE * SIDE, 4, 2 * DEPTH, QUART), bf16),
            pltpu.VMEM((4, 2 * ROWS, QUART), f32),
            pltpu.VMEM((4, ROWS, QUART), bf16),
            pltpu.VMEM((layers, depth, wide), bf16),
            pltpu.VMEM((REPLICAS, layers, depth, COLS), bf16),
            pltpu.VMEM((layers, depth, COLS), f32),
            pltpu.VMEM((layers, depth, COLS), f32),
            pltpu.VMEM((REPLICAS, layers, depth, COLS), bf16),
            pltpu.VMEM((4, 4, 8, 128), f32),
            dma((4, STEPS + 2)),
            dma((4, STEPS + 2)),
            dma((16,)),
            dma((16,)),
            dma((16,)),
            dma((4,)),
            dma((4,)),
            dma((4,)),
            dma((3,)),
            dma((3,)),
            dma((3,)),
            dma((3,)),
            dma((4, 3)),
            dma((4, 3)),
            dma((4,)),
            dma((4,)),
            dma((4,)),
        ],
        compiler_params=pltpu.CompilerParams(
            collective_id=0, has_side_effects=True, vmem_limit_bytes=52 * 1024 * 1024
        ),
    )(tokens, next_weights, inner_weights, global_weights, momentum)
    held = [pltpu.with_memory_space_constraint(array, pltpu.VMEM) for array in held]
    return pl.pallas_call(
        write_out,
        name="write_out",
        out_shape=tuple(jax.ShapeDtypeStruct(*result) for result in results),
        in_specs=[vmem] * 6,
        out_specs=(any_,) * 6,
        scratch_shapes=[dma((6,))],
        compiler_params=pltpu.CompilerParams(vmem_limit_bytes=8 * 1024 * 1024),
    )(*held)


def solution(mesh):
    placed = (
        P("replica", "fsdp", None),
        P("replica", "fsdp", None),
        P("replica", None, "fsdp", None),
        P(None, "fsdp", "replica"),
        P(None, "fsdp", "replica"),
    )
    return jax.shard_map(
        on_device,
        mesh=mesh,
        in_specs=placed,
        out_specs=(
            P("replica", "fsdp", None),
            P(None, "fsdp", "replica"),
            P(None, "fsdp", "replica"),
            P(None, "fsdp", "replica"),
            P("replica", None, "fsdp", None),
            P(),
        ),
        check_vma=False,
    )
```

```python
import functools

import jax
import jax.numpy as jnp
from jax import lax
from jax.experimental import pallas as pl
from jax.experimental.pallas import tpu as pltpu
from jax.sharding import PartitionSpec as P

MESH = pl.DeviceIdType.MESH
KVW = 1024
SIDE = 4
REPLICAS = 4
DEPTH = 256
QUART = 256
ROWS = 512
COLS = 512
STEPS = 15
AHEAD = 3
REUSE = 2 * AHEAD
CHUNK = 512
outer_rate = 0.7
outer_mom = 0.9
mix_share = 0.5


def build_queues():
    def place(axis, along, across):
        return (along, across) if axis == 0 else (across, along)

    queues = {}
    for axis in (0, 1):
        first = (0, 1) if axis == 0 else (2, 3)
        late = (2, 3) if axis == 0 else (0, 1)
        for sign in (1, -1):
            via, other = (first, late) if sign == 1 else (first[::-1], late[::-1])
            items = [(via[0], 0, 0), (via[1], 0, 0), (other[0], 0, 0), (other[1], 0, 0)]
            items += [(via[0],) + place(axis, -sign, 0)]
            items += [(quarter,) + place(axis, 0, across) for quarter in other for across in (-1, 1)]
            ends = [(quarter,) + place(axis, 0, 2) for quarter in other]
            passed = [(other[0],) + place(axis, -sign, across) for across in (0, -1, 1, 2)]
            items += ends + passed if sign == 1 else ends[:1] + passed + ends[1:]
            queues[axis, sign] = items
    return queues


QUEUES = build_queues()
WAYS = ((0, 1), (0, -1), (1, 1), (1, -1))


def arrivals(step):
    found = []
    for axis, sign in WAYS:
        quarter, ox, oy = QUEUES[axis, sign][step]
        found.append((quarter, ox - sign, oy) if axis == 0 else (quarter, ox, oy - sign))
    return [(quarter, ox % SIDE, oy % SIDE) for quarter, ox, oy in found]


def kernel(
    tokens,
    weights,
    inner,
    outer_in,
    momentum_in,
    projected,
    new_global,
    new_momentum,
    normalized,
    mixed,
    amax_out,
    tok,
    wts,
    acc,
    out_far,
    out_here,
    inner_v,
    parts,
    outer_v,
    momentum_v,
    normal_v,
    amax_v,
    full,
    peaks,
    ring_send,
    ring_recv,
    tok_here,
    tok_send,
    tok_recv,
    wts_here,
    wts_send,
    wts_recv,
    sum_send,
    sum_recv,
    full_send,
    full_recv,
    peak_send,
    peak_recv,
    out_send,
    out_recv,
    local_sem,
    result_sem,
):
    rep = lax.axis_index("replica")
    fsdp = lax.axis_index("fsdp")
    core = fsdp % 2
    x = (fsdp // 2) % SIDE
    y = fsdp // (2 * SIDE)

    def chip_at(ox, oy):
        return ((y + oy) % SIDE) * SIDE + (x + ox) % SIDE

    def at_plane(ox, oy):
        return {"replica": rep, "fsdp": chip_at(ox, oy) * 2 + core}

    def at_replica(oz):
        return {"replica": (rep + oz) % REPLICAS, "fsdp": fsdp}

    sibling = {"replica": rep, "fsdp": chip_at(0, 0) * 2 + 1 - core}
    me = chip_at(0, 0)

    def remote(src, dst, send, recv, device):
        return pltpu.make_async_remote_copy(
            src_ref=src, dst_ref=dst, send_sem=send, recv_sem=recv, device_id=device, device_id_type=MESH
        )

    my_rows = pl.ds(pl.multiple_of(core * ROWS, ROWS), ROWS)
    my_depth = pl.ds(pl.multiple_of(core * DEPTH, DEPTH), DEPTH)

    def columns(which, quarter):
        return pl.ds(pl.multiple_of(which * KVW + quarter * QUART, QUART), QUART)

    def start_local(src, dst, sem):
        copy = pltpu.make_async_copy(src, dst, sem)
        copy.start()
        return copy

    w_here = [
        start_local(weights.at[0, :, columns(core, q)], wts.at[me, q, my_depth, :], wts_here.at[q]) for q in range(4)
    ]

    barrier = pltpu.get_barrier_semaphore()
    peers = [sibling] + [at_plane(o, 0) for o in (1, 3)] + [at_plane(0, o) for o in (1, 3)]
    peers += [at_replica(o) for o in (1, 3)]
    for peer in peers:
        pl.semaphore_signal(barrier, inc=1, device_id=peer, device_id_type=MESH)
    pl.semaphore_wait(barrier, len(peers))

    def ring_copy(way, step):
        axis, sign = WAYS[way]
        quarter, ox, oy = QUEUES[axis, sign][step]
        device = at_plane(sign, 0) if axis == 0 else at_plane(0, sign)
        block = wts.at[chip_at(ox, oy), quarter]
        if step > 1:
            return [remote(block, block, ring_send.at[way, step % AHEAD], ring_recv.at[way, step % REUSE], device)]
        copies = []
        for half, which in enumerate((core, 1 - core)):
            part = wts.at[me, quarter, pl.ds(pl.multiple_of(which * DEPTH, DEPTH), DEPTH), :]
            src = weights.at[0, :, columns(core, quarter)] if half == 0 else part
            send = ring_send.at[way, step if half == 0 else AHEAD + step]
            recv = ring_recv.at[way, step if half == 0 else REUSE + step]
            copies.append(remote(src, part, send, recv, device))
        return copies

    ring = {(way, step): ring_copy(way, step) for way in range(4) for step in range(AHEAD)}
    for step in (0, 1):
        for way in range(4):
            ring[way, step][0].start()

    w_far = []
    for q in range(4):
        copy = remote(
            weights.at[0, :, columns(1 - core, q)], wts.at[me, q, my_depth, :], wts_send.at[q], wts_recv.at[q], sibling
        )
        copy.start()
        w_far.append(copy)

    def sum_copy(oz):
        target = (rep + oz) % REPLICAS
        return remote(
            inner.at[0, :, :, pl.ds(pl.multiple_of(target * COLS, COLS), COLS)],
            parts.at[rep],
            sum_send.at[oz - 1],
            sum_recv.at[oz - 1],
            at_replica(oz),
        )

    sums = [sum_copy(oz) for oz in (1, 2, 3)]
    sums[0].start()
    sums[2].start()

    for copy in w_here:
        copy.wait()
    for copy in w_far:
        copy.wait_recv()
    for step in range(AHEAD):
        for way in range(4):
            ring[way, step][-1].start()

    tok_copies = {}
    for n, oy in enumerate((0, 3, 1, 2)):
        line = (y + oy) % SIDE
        width = SIDE * 2 * DEPTH
        src = tokens.at[0, :, pl.ds(pl.multiple_of(line * width, width), width)]
        dst = tok.at[line, my_rows, :]
        here = start_local(src, dst, tok_here.at[n])
        far = remote(src, dst, tok_send.at[n], tok_recv.at[n], sibling)
        far.start()
        tok_copies[oy] = (here, far)

    own_cols = pl.ds(pl.multiple_of(rep * COLS, COLS), COLS)
    outer_copies = [
        start_local(outer_in, outer_v, local_sem.at[0]),
        start_local(momentum_in, momentum_v, local_sem.at[1]),
        start_local(inner.at[0, :, :, own_cols], parts.at[rep], local_sem.at[2]),
        start_local(inner.at[0], inner_v, local_sem.at[3]),
    ]

    have = set()

    def need_tokens(spots):
        for spot in spots:
            if spot not in have:
                have.add(spot)
                here, far = tok_copies[spot]
                here.wait()
                far.wait_recv()

    def pick(i, values):
        result = values[0]
        for n in range(1, len(values)):
            result = jnp.where(i == n, values[n], result)
        return result

    chunks = 2 * ROWS // CHUNK

    def product(rows, ox, oy, quarter):
        cols = pl.ds(pl.multiple_of(ox * 2 * DEPTH, 2 * DEPTH), 2 * DEPTH)
        return jnp.dot(tok[oy, rows, cols], wts[oy * SIDE + ox, quarter], preferred_element_type=jnp.float32)

    def owner(ox, oy):
        return (x + ox) % SIDE, (y + oy) % SIDE

    def multiply(items, first):
        need_tokens([oy for _, _, oy in items])
        quarters = [q for q, _, _ in items]
        lines = [owner(ox, oy) for _, ox, oy in items]

        def body(i, carry):
            n, m = i // chunks, i % chunks
            quarter = pick(n, quarters)
            ox, oy = pick(n, [line[0] for line in lines]), pick(n, [line[1] for line in lines])
            rows = pl.ds(pl.multiple_of(m * CHUNK, CHUNK), CHUNK)
            part = product(rows, ox, oy, quarter)
            if first:
                acc[quarter, rows, :] = part
            else:
                acc[quarter, rows, :] += part
            return carry

        lax.fori_loop(0, len(items) * chunks, body, 0)

    other_rows = pl.ds(pl.multiple_of((1 - core) * ROWS, ROWS), ROWS)
    out_copies = []

    def finish(items):
        for rows, stage in ((other_rows, out_far), (my_rows, out_here)):
            for q in items:
                value = acc[q, rows, :]
                for ox, oy in items[q]:
                    value += product(rows, *owner(ox, oy), q)
                stage[q] = value.astype(jnp.bfloat16)
                place = projected.at[0, :, columns(core, q)]
                if stage is out_far:
                    copy = remote(stage.at[q], place, out_send.at[q], out_recv.at[q], sibling)
                    copy.start()
                else:
                    copy = start_local(stage.at[q], place, result_sem.at[q])
                out_copies.append(copy)

    LINES = 32
    is_value = rep // 2

    results = []

    def update():
        for copy in outer_copies[:3]:
            copy.wait()
        sums[1].wait_recv()
        highest = []
        for layer in range(2):

            def body(i, carry, layer=layer):
                rows = pl.ds(pl.multiple_of(i * LINES, LINES), LINES)
                total = parts[0, layer, rows, :].astype(jnp.float32)
                for r in range(1, REPLICAS):
                    total += parts[r, layer, rows, :].astype(jnp.float32)
                outer = outer_v[layer, rows, :]
                pseudo = outer - total / REPLICAS
                moved = outer_mom * momentum_v[layer, rows, :] + pseudo
                stepped = outer - outer_rate * (pseudo + outer_mom * moved)
                momentum_v[layer, rows, :] = moved
                outer_v[layer, rows, :] = stepped
                full[rep, layer, rows, :] = stepped.astype(jnp.bfloat16)
                return jnp.maximum(carry, jnp.abs(stepped))

            top = lax.fori_loop(0, DEPTH // LINES, body, jnp.zeros((LINES, COLS), jnp.float32))
            highest.append(jnp.max(jnp.max(top, axis=0, keepdims=True), axis=1, keepdims=True))
        results.append(start_local(momentum_v, new_momentum, result_sem.at[4]))
        results.append(start_local(outer_v, new_global, result_sem.at[5]))
        line = lax.broadcasted_iota(jnp.int32, (8, 128), 0)
        tile = jnp.where(
            line == is_value, highest[0], jnp.where(line == 2 + is_value, highest[1], jnp.zeros((8, 128), jnp.float32))
        )
        peak_copies[0] = send_peaks(0, tile)
        copies = []
        for oz in (1, 2, 3):
            copy = remote(
                full.at[rep], full.at[rep], full_send.at[oz - 1], full_recv.at[oz - 1], at_replica(oz)
            )
            copy.start()
            copies.append(copy)
        return copies

    def send_peaks(stage, tile):
        peaks[stage, 0] = tile
        if stage == 3:
            devices = [sibling]
        else:
            devices = [(at_replica(o), at_plane(0, o), at_plane(o, 0))[stage] for o in (1, 2, 3)]
        copies = []
        for n, device in enumerate(devices):
            copy = remote(
                peaks.at[stage, 0], peaks.at[stage, n + 1], peak_send.at[n], peak_recv.at[stage, n], device
            )
            copy.start()
            copies.append(copy)
        return copies

    def take_peaks(stage, copies):
        for copy in copies:
            copy.wait()
        tile = peaks[stage, 0]
        for n in range(len(copies)):
            tile = jnp.maximum(tile, peaks[stage, n + 1])
        return tile

    def normalize(tile):
        values = [[tile[2 * l + t : 2 * l + t + 1, 0:1] for t in range(2)] for l in range(2)]
        row = lax.broadcasted_iota(jnp.int32, (2, 2), 0)
        col = lax.broadcasted_iota(jnp.int32, (2, 2), 1)
        amax_v[...] = jnp.where(
            row == 0,
            jnp.where(col == 0, values[0][0], values[0][1]),
            jnp.where(col == 0, values[1][0], values[1][1]),
        )
        for layer in range(2):
            scale = jnp.where(is_value == 0, values[layer][0], values[layer][1]) + 1e-06

            def body(i, carry, layer=layer, scale=scale):
                rows = pl.ds(pl.multiple_of(i * LINES, LINES), LINES)
                normal_v[layer, rows, :] = (outer_v[layer, rows, :] / scale).astype(jnp.bfloat16)
                return carry

            lax.fori_loop(0, DEPTH // LINES, body, 0)
        results.append(start_local(normal_v, normalized, result_sem.at[6]))
        results.append(start_local(amax_v, amax_out, result_sem.at[7]))

    def mix(copies):
        outer_copies[3].wait()
        for copy in copies:
            copy.wait_recv()

        def body(i, carry):
            layer, n = i // (DEPTH // LINES), i % (DEPTH // LINES)
            rows = pl.ds(pl.multiple_of(n * LINES, LINES), LINES)
            for r in range(REPLICAS):
                cols = slice(r * COLS, (r + 1) * COLS)
                value = mix_share * inner_v[layer, rows, cols].astype(jnp.float32)
                value += (1.0 - mix_share) * full[r, layer, rows, :].astype(jnp.float32)
                inner_v[layer, rows, cols] = value.astype(jnp.bfloat16)
            return carry

        lax.fori_loop(0, 2 * DEPTH // LINES, body, 0)
        results.append(start_local(inner_v, mixed.at[0], result_sem.at[8]))

    multiply([(q, 0, 0) for q in range(4)], True)
    peak_copies = {}
    full_copies = []
    for step in range(STEPS):
        for way in range(4):
            for copy in ring[way, step]:
                copy.wait_recv()
        if step + AHEAD < STEPS:
            for way in range(4):
                for copy in ring[way, step]:
                    copy.wait_send()
                ring[way, step + AHEAD] = ring_copy(way, step + AHEAD)
                ring[way, step + AHEAD][0].start()
        if step < STEPS - 1:
            multiply(arrivals(step), False)
        if step == STEPS - 2:
            finish({1: [], 3: []})
        if step == 1:
            sums[0].wait_recv()
            sums[2].wait_recv()
            sums[1].start()
        if step == 4:
            full_copies = update()
        if step in (6, 8, 10):
            stage = step // 2 - 3
            tile = take_peaks(stage, peak_copies[stage])
            peak_copies[stage + 1] = send_peaks(stage + 1, tile)
        if step == 11:
            normalize(take_peaks(3, peak_copies[3]))
        if step == 12:
            mix(full_copies)

    last = {}
    for q, ox, oy in arrivals(STEPS - 1):
        last.setdefault(q, []).append((ox, oy))
    need_tokens([oy for items in last.values() for _, oy in items])
    finish(last)

    for way in range(4):
        for step in range(STEPS - AHEAD, STEPS):
            ring[way, step][0].wait_send()
    for copy in w_far + sums + full_copies + [far for _, far in tok_copies.values()]:
        copy.wait_send()
    for copy in out_copies + results:
        copy.wait()


def write_out(*refs):
    n = len(refs) // 2
    sem = refs[-1]
    copies = [pltpu.make_async_copy(refs[i], refs[n + i], sem.at[i]) for i in range(n)]
    for copy in copies:
        copy.start()
    for copy in copies:
        copy.wait()


def on_device(tokens, next_weights, inner_weights, global_weights, momentum):
    bf16, f32 = jnp.bfloat16, jnp.float32
    dma = pltpu.SemaphoreType.DMA
    any_ = pl.BlockSpec(memory_space=pl.ANY)
    layers, depth, wide = inner_weights.shape[1:]
    results = (
        ((1, ROWS, 2 * KVW), bf16),
        ((layers, depth, COLS), f32),
        ((layers, depth, COLS), f32),
        ((layers, depth, COLS), bf16),
        ((1, layers, depth, wide), bf16),
        ((2, 2), f32),
    )
    held = pl.pallas_call(
        kernel,
        name="project_and_outer_step",
        out_shape=tuple(pltpu.VMEM(*result) for result in results),
        in_specs=[any_] * 5,
        out_specs=(any_,) * 6,
        scratch_shapes=[
            pltpu.VMEM((SIDE, 2 * ROWS, SIDE * 2 * DEPTH), bf16),
            pltpu.VMEM((SIDE * SIDE, 4, 2 * DEPTH, QUART), bf16),
            pltpu.VMEM((4, 2 * ROWS, QUART), f32),
            pltpu.VMEM((4, ROWS, QUART), bf16),
            pltpu.VMEM((4, ROWS, QUART), bf16),
            pltpu.VMEM((layers, depth, wide), bf16),
            pltpu.VMEM((REPLICAS, layers, depth, COLS), bf16),
            pltpu.VMEM((layers, depth, COLS), f32),
            pltpu.VMEM((layers, depth, COLS), f32),
            pltpu.VMEM((layers, depth, COLS), bf16),
            pltpu.VMEM((2, 2), f32),
            pltpu.VMEM((REPLICAS, layers, depth, COLS), bf16),
            pltpu.VMEM((4, 4, 8, 128), f32),
            dma((4, AHEAD + 2)),
            dma((4, REUSE + 2)),
            dma((4,)),
            dma((4,)),
            dma((4,)),
            dma((4,)),
            dma((4,)),
            dma((4,)),
            dma((3,)),
            dma((3,)),
            dma((3,)),
            dma((3,)),
            dma((3,)),
            dma((4, 3)),
            dma((4,)),
            dma((4,)),
            dma((4,)),
            dma((9,)),
        ],
        compiler_params=pltpu.CompilerParams(
            collective_id=0, has_side_effects=True, vmem_limit_bytes=52 * 1024 * 1024
        ),
    )(tokens, next_weights, inner_weights, global_weights, momentum)
    held = [pltpu.with_memory_space_constraint(array, pltpu.VMEM) for array in held]
    return pl.pallas_call(
        write_out,
        name="write_out",
        out_shape=tuple(jax.ShapeDtypeStruct(*result) for result in results),
        in_specs=[any_] * 6,
        out_specs=(any_,) * 6,
        scratch_shapes=[dma((6,))],
        compiler_params=pltpu.CompilerParams(vmem_limit_bytes=8 * 1024 * 1024),
    )(*held)


def solution(mesh):
    placed = (
        P("replica", "fsdp", None),
        P("replica", "fsdp", None),
        P("replica", None, "fsdp", None),
        P(None, "fsdp", "replica"),
        P(None, "fsdp", "replica"),
    )
    return jax.shard_map(
        on_device,
        mesh=mesh,
        in_specs=placed,
        out_specs=(
            P("replica", "fsdp", None),
            P(None, "fsdp", "replica"),
            P(None, "fsdp", "replica"),
            P(None, "fsdp", "replica"),
            P("replica", None, "fsdp", None),
            P(),
        ),
        check_vma=False,
    )
```

```python
import functools

import jax
import jax.numpy as jnp
from jax import lax
from jax.experimental import pallas as pl
from jax.experimental.pallas import tpu as pltpu
from jax.sharding import PartitionSpec as P

MESH = pl.DeviceIdType.MESH
KVW = 1024
SIDE = 4
REPLICAS = 4
DEPTH = 256
QUART = 256
ROWS = 512
COLS = 512
STEPS = 15
AHEAD = 3
REUSE = 2 * AHEAD
CHUNK = 512
outer_rate = 0.7
outer_mom = 0.9
mix_share = 0.5


def build_queues():
    def place(axis, along, across):
        return (along, across) if axis == 0 else (across, along)

    queues = {}
    for axis in (0, 1):
        first = (0, 1) if axis == 0 else (2, 3)
        late = (2, 3) if axis == 0 else (0, 1)
        for sign in (1, -1):
            via, other = (first, late) if sign == 1 else (first[::-1], late[::-1])
            items = [(via[0], 0, 0), (via[1], 0, 0), (other[0], 0, 0), (other[1], 0, 0)]
            items += [(via[0],) + place(axis, -sign, 0)]
            items += [(quarter,) + place(axis, 0, across) for quarter in other for across in (-1, 1)]
            ends = [(quarter,) + place(axis, 0, 2) for quarter in other]
            passed = [(other[0],) + place(axis, -sign, across) for across in (0, -1, 1, 2)]
            items += ends + passed if sign == 1 else ends[:1] + passed + ends[1:]
            queues[axis, sign] = items
    return queues


QUEUES = build_queues()
WAYS = ((0, 1), (0, -1), (1, 1), (1, -1))


def arrivals(step):
    found = []
    for axis, sign in WAYS:
        quarter, ox, oy = QUEUES[axis, sign][step]
        found.append((quarter, ox - sign, oy) if axis == 0 else (quarter, ox, oy - sign))
    return [(quarter, ox % SIDE, oy % SIDE) for quarter, ox, oy in found]


def kernel(
    tokens,
    weights,
    inner,
    outer_in,
    momentum_in,
    projected,
    new_global,
    new_momentum,
    normalized,
    mixed,
    amax_out,
    tok,
    wts,
    acc,
    out_stage,
    inner_v,
    parts,
    outer_v,
    momentum_v,
    normal_v,
    amax_v,
    full,
    peaks,
    ring_send,
    ring_recv,
    tok_here,
    tok_send,
    tok_recv,
    wts_here,
    wts_send,
    wts_recv,
    sum_send,
    sum_recv,
    full_send,
    full_recv,
    peak_send,
    peak_recv,
    out_send,
    out_recv,
    local_sem,
    result_sem,
    greet,
):
    rep = lax.axis_index("replica")
    fsdp = lax.axis_index("fsdp")
    core = fsdp % 2
    x = (fsdp // 2) % SIDE
    y = fsdp // (2 * SIDE)

    def chip_at(ox, oy):
        return ((y + oy) % SIDE) * SIDE + (x + ox) % SIDE

    def at_plane(ox, oy):
        return {"replica": rep, "fsdp": chip_at(ox, oy) * 2 + core}

    def at_replica(oz):
        return {"replica": (rep + oz) % REPLICAS, "fsdp": fsdp}

    sibling = {"replica": rep, "fsdp": chip_at(0, 0) * 2 + 1 - core}
    me = chip_at(0, 0)

    def remote(src, dst, send, recv, device):
        return pltpu.make_async_remote_copy(
            src_ref=src, dst_ref=dst, send_sem=send, recv_sem=recv, device_id=device, device_id_type=MESH
        )

    my_rows = pl.ds(pl.multiple_of(core * ROWS, ROWS), ROWS)
    my_depth = pl.ds(pl.multiple_of(core * DEPTH, DEPTH), DEPTH)

    def columns(which, quarter):
        return pl.ds(pl.multiple_of(which * KVW + quarter * QUART, QUART), QUART)

    def start_local(src, dst, sem):
        copy = pltpu.make_async_copy(src, dst, sem)
        copy.start()
        return copy

    w_here = [
        start_local(weights.at[0, :, columns(core, q)], wts.at[me, q, my_depth, :], wts_here.at[q]) for q in range(4)
    ]

    def signal(sem, device):
        pl.semaphore_signal(sem, inc=1, device_id=device, device_id_type=MESH)

    barrier = pltpu.get_barrier_semaphore()
    plane = [sibling] + [at_plane(o, 0) for o in (1, 3)] + [at_plane(0, o) for o in (1, 3)]
    for peer in plane:
        signal(barrier, peer)
    first, last_rep = rep == 0, rep == REPLICAS - 1

    @pl.when(jnp.logical_not(last_rep))
    def _():
        signal(barrier, at_replica(1))

    @pl.when(first)
    def _():
        signal(barrier, at_replica(REPLICAS - 1))

    pl.semaphore_wait(barrier, len(plane) + jnp.minimum(rep, 1) + rep // (REPLICAS - 1))

    @pl.when(jnp.logical_not(first))
    def _():
        signal(greet, at_replica(REPLICAS - 1))

    @pl.when(last_rep)
    def _():
        signal(greet, at_replica(1))

    def ring_copy(way, step):
        axis, sign = WAYS[way]
        quarter, ox, oy = QUEUES[axis, sign][step]
        device = at_plane(sign, 0) if axis == 0 else at_plane(0, sign)
        block = wts.at[chip_at(ox, oy), quarter]
        if step > 1:
            return [remote(block, block, ring_send.at[way, step % AHEAD], ring_recv.at[way, step % REUSE], device)]
        copies = []
        for half, which in enumerate((core, 1 - core)):
            part = wts.at[me, quarter, pl.ds(pl.multiple_of(which * DEPTH, DEPTH), DEPTH), :]
            src = weights.at[0, :, columns(core, quarter)] if half == 0 else part
            send = ring_send.at[way, step if half == 0 else AHEAD + step]
            recv = ring_recv.at[way, step if half == 0 else REUSE + step]
            copies.append(remote(src, part, send, recv, device))
        return copies

    ring = {(way, step): ring_copy(way, step) for way in range(4) for step in range(AHEAD)}
    for step in (0, 1):
        for way in range(4):
            ring[way, step][0].start()

    w_far = []
    for q in range(4):
        copy = remote(
            weights.at[0, :, columns(1 - core, q)], wts.at[me, q, my_depth, :], wts_send.at[q], wts_recv.at[q], sibling
        )
        copy.start()
        w_far.append(copy)

    def sum_copy(oz):
        target = (rep + oz) % REPLICAS
        return remote(
            inner.at[0, :, :, pl.ds(pl.multiple_of(target * COLS, COLS), COLS)],
            parts.at[rep],
            sum_send.at[oz - 1],
            sum_recv.at[oz - 1],
            at_replica(oz),
        )

    sums = [sum_copy(oz) for oz in (1, 2, 3)]
    for copy in w_here:
        copy.wait()
    for copy in w_far:
        copy.wait_recv()
    for step in range(AHEAD):
        for way in range(4):
            ring[way, step][-1].start()

    tok_copies = {}
    for n, oy in enumerate((0, 3, 1, 2)):
        line = (y + oy) % SIDE
        width = SIDE * 2 * DEPTH
        src = tokens.at[0, :, pl.ds(pl.multiple_of(line * width, width), width)]
        dst = tok.at[line, my_rows, :]
        here = start_local(src, dst, tok_here.at[n])
        far = remote(src, dst, tok_send.at[n], tok_recv.at[n], sibling)
        far.start()
        tok_copies[oy] = (here, far)

    own_cols = pl.ds(pl.multiple_of(rep * COLS, COLS), COLS)
    outer_copies = [
        start_local(outer_in, outer_v, local_sem.at[0]),
        start_local(momentum_in, momentum_v, local_sem.at[1]),
        start_local(inner.at[0, :, :, own_cols], parts.at[rep], local_sem.at[2]),
        start_local(inner.at[0], inner_v, local_sem.at[3]),
    ]

    @pl.when(jnp.logical_not(last_rep))
    def _():
        pl.semaphore_wait(greet, 2 - jnp.minimum(rep, 1))

    sums[0].start()
    sums[2].start()

    have = set()

    def need_tokens(spots):
        for spot in spots:
            if spot not in have:
                have.add(spot)
                here, far = tok_copies[spot]
                here.wait()
                far.wait_recv()

    def pick(i, values):
        result = values[0]
        for n in range(1, len(values)):
            result = jnp.where(i == n, values[n], result)
        return result

    chunks = 2 * ROWS // CHUNK

    def product(rows, ox, oy, quarter):
        cols = pl.ds(pl.multiple_of(ox * 2 * DEPTH, 2 * DEPTH), 2 * DEPTH)
        return jnp.dot(tok[oy, rows, cols], wts[oy * SIDE + ox, quarter], preferred_element_type=jnp.float32)

    def owner(ox, oy):
        return (x + ox) % SIDE, (y + oy) % SIDE

    def multiply(items, first):
        need_tokens([oy for _, _, oy in items])
        quarters = [q for q, _, _ in items]
        lines = [owner(ox, oy) for _, ox, oy in items]

        def body(i, carry):
            n, m = i // chunks, i % chunks
            quarter = pick(n, quarters)
            ox, oy = pick(n, [line[0] for line in lines]), pick(n, [line[1] for line in lines])
            rows = pl.ds(pl.multiple_of(m * CHUNK, CHUNK), CHUNK)
            part = product(rows, ox, oy, quarter)
            if first:
                acc[quarter, rows, :] = part
            else:
                acc[quarter, rows, :] += part
            return carry

        lax.fori_loop(0, len(items) * chunks, body, 0)

    def out_copy(half, q):
        place = projected.at[0, :, columns(core, q)]
        if half == 0:
            return remote(out_stage.at[0, q], place, out_send.at[q], out_recv.at[q], sibling)
        return pltpu.make_async_copy(out_stage.at[1, q], place, result_sem.at[q])

    def finish(items):
        quarters = list(items)
        lines = [[owner(ox, oy) for ox, oy in items[q]] for q in quarters]

        def body(i, carry):
            half, n = i // len(quarters), i % len(quarters)
            q = pick(n, quarters)
            rows = pl.ds(pl.multiple_of(jnp.where(half == 0, 1 - core, core) * ROWS, ROWS), ROWS)
            value = acc[q, rows, :]
            for spot in range(len(lines[0])):
                ox, oy = (pick(n, [line[spot][axis] for line in lines]) for axis in (0, 1))
                value += product(rows, ox, oy, q)
            out_stage[half, q] = value.astype(jnp.bfloat16)

            @pl.when(half == 0)
            def _():
                out_copy(0, q).start()

            @pl.when(half == 1)
            def _():
                out_copy(1, q).start()

            return carry

        lax.fori_loop(0, 2 * len(quarters), body, 0)

    LINES = 32
    is_value = rep // 2

    results = []

    def update():
        for copy in outer_copies[:3]:
            copy.wait()
        sums[1].wait_recv()
        highest = []
        for layer in range(2):

            def body(i, carry, layer=layer):
                rows = pl.ds(pl.multiple_of(i * LINES, LINES), LINES)
                total = parts[0, layer, rows, :].astype(jnp.float32)
                for r in range(1, REPLICAS):
                    total += parts[r, layer, rows, :].astype(jnp.float32)
                outer = outer_v[layer, rows, :]
                pseudo = outer - total / REPLICAS
                moved = outer_mom * momentum_v[layer, rows, :] + pseudo
                stepped = outer - outer_rate * (pseudo + outer_mom * moved)
                momentum_v[layer, rows, :] = moved
                outer_v[layer, rows, :] = stepped
                full[rep, layer, rows, :] = stepped.astype(jnp.bfloat16)
                return jnp.maximum(carry, jnp.abs(stepped))

            top = lax.fori_loop(0, DEPTH // LINES, body, jnp.zeros((LINES, COLS), jnp.float32))
            highest.append(jnp.max(jnp.max(top, axis=0, keepdims=True), axis=1, keepdims=True))
        results.append(start_local(momentum_v, new_momentum, result_sem.at[4]))
        results.append(start_local(outer_v, new_global, result_sem.at[5]))
        line = lax.broadcasted_iota(jnp.int32, (8, 128), 0)
        tile = jnp.where(
            line == is_value, highest[0], jnp.where(line == 2 + is_value, highest[1], jnp.zeros((8, 128), jnp.float32))
        )
        peak_copies[0] = send_peaks(0, tile)
        copies = []
        for oz in (1, 2, 3):
            copy = remote(
                full.at[rep], full.at[rep], full_send.at[oz - 1], full_recv.at[oz - 1], at_replica(oz)
            )
            copy.start()
            copies.append(copy)
        return copies

    def send_peaks(stage, tile):
        peaks[stage, 0] = tile
        if stage == 3:
            devices = [sibling]
        else:
            devices = [(at_replica(o), at_plane(0, o), at_plane(o, 0))[stage] for o in (1, 2, 3)]
        copies = []
        for n, device in enumerate(devices):
            copy = remote(
                peaks.at[stage, 0], peaks.at[stage, n + 1], peak_send.at[n], peak_recv.at[stage, n], device
            )
            copy.start()
            copies.append(copy)
        return copies

    def take_peaks(stage, copies):
        for copy in copies:
            copy.wait()
        tile = peaks[stage, 0]
        for n in range(len(copies)):
            tile = jnp.maximum(tile, peaks[stage, n + 1])
        return tile

    def normalize(tile):
        values = [[tile[2 * l + t : 2 * l + t + 1, 0:1] for t in range(2)] for l in range(2)]
        row = lax.broadcasted_iota(jnp.int32, (2, 2), 0)
        col = lax.broadcasted_iota(jnp.int32, (2, 2), 1)
        amax_v[...] = jnp.where(
            row == 0,
            jnp.where(col == 0, values[0][0], values[0][1]),
            jnp.where(col == 0, values[1][0], values[1][1]),
        )
        for layer in range(2):
            scale = jnp.where(is_value == 0, values[layer][0], values[layer][1]) + 1e-06

            def body(i, carry, layer=layer, scale=scale):
                rows = pl.ds(pl.multiple_of(i * LINES, LINES), LINES)
                normal_v[layer, rows, :] = (outer_v[layer, rows, :] / scale).astype(jnp.bfloat16)
                return carry

            lax.fori_loop(0, DEPTH // LINES, body, 0)
        results.append(start_local(normal_v, normalized, result_sem.at[6]))
        results.append(start_local(amax_v, amax_out, result_sem.at[7]))

    def mix(copies):
        outer_copies[3].wait()
        for copy in copies:
            copy.wait_recv()

        def body(i, carry):
            layer, n = i // (DEPTH // LINES), i % (DEPTH // LINES)
            rows = pl.ds(pl.multiple_of(n * LINES, LINES), LINES)
            for r in range(REPLICAS):
                cols = slice(r * COLS, (r + 1) * COLS)
                value = mix_share * inner_v[layer, rows, cols].astype(jnp.float32)
                value += (1.0 - mix_share) * full[r, layer, rows, :].astype(jnp.float32)
                inner_v[layer, rows, cols] = value.astype(jnp.bfloat16)
            return carry

        lax.fori_loop(0, 2 * DEPTH // LINES, body, 0)
        results.append(start_local(inner_v, mixed.at[0], result_sem.at[8]))

    multiply([(q, 0, 0) for q in range(4)], True)
    peak_copies = {}
    full_copies = []
    for step in range(STEPS):
        for way in range(4):
            for copy in ring[way, step]:
                copy.wait_recv()
        if step + AHEAD < STEPS:
            for way in range(4):
                for copy in ring[way, step]:
                    copy.wait_send()
                ring[way, step + AHEAD] = ring_copy(way, step + AHEAD)
                ring[way, step + AHEAD][0].start()
        if step < STEPS - 1:
            multiply(arrivals(step), False)
        if step == STEPS - 2:
            finish({1: [], 3: []})
        if step == 2:
            sums[0].wait_recv()
            sums[2].wait_recv()
            sums[1].start()
        if step == 5:
            full_copies = update()
        if step in (7, 9, 11):
            stage = (step - 7) // 2
            tile = take_peaks(stage, peak_copies[stage])
            peak_copies[stage + 1] = send_peaks(stage + 1, tile)
        if step == 12:
            normalize(take_peaks(3, peak_copies[3]))
        if step == 12:
            mix(full_copies)

    last = {}
    for q, ox, oy in arrivals(STEPS - 1):
        last.setdefault(q, []).append((ox, oy))
    need_tokens([oy for items in last.values() for _, oy in items])
    finish(last)

    for way in range(4):
        for step in range(STEPS - AHEAD, STEPS):
            ring[way, step][0].wait_send()
    for copy in w_far + sums + full_copies + [far for _, far in tok_copies.values()]:
        copy.wait_send()
    for copy in [out_copy(half, q) for half in (0, 1) for q in range(4)] + results:
        copy.wait()


def write_out(*refs):
    n = len(refs) // 2
    sem = refs[-1]
    copies = [pltpu.make_async_copy(refs[i], refs[n + i], sem.at[i]) for i in range(n)]
    for copy in copies:
        copy.start()
    for copy in copies:
        copy.wait()


def on_device(tokens, next_weights, inner_weights, global_weights, momentum):
    bf16, f32 = jnp.bfloat16, jnp.float32
    dma = pltpu.SemaphoreType.DMA
    any_ = pl.BlockSpec(memory_space=pl.ANY)
    layers, depth, wide = inner_weights.shape[1:]
    results = (
        ((1, ROWS, 2 * KVW), bf16),
        ((layers, depth, COLS), f32),
        ((layers, depth, COLS), f32),
        ((layers, depth, COLS), bf16),
        ((1, layers, depth, wide), bf16),
        ((2, 2), f32),
    )
    held = pl.pallas_call(
        kernel,
        name="project_and_outer_step",
        out_shape=tuple(pltpu.VMEM(*result) for result in results),
        in_specs=[any_] * 5,
        out_specs=(any_,) * 6,
        scratch_shapes=[
            pltpu.VMEM((SIDE, 2 * ROWS, SIDE * 2 * DEPTH), bf16),
            pltpu.VMEM((SIDE * SIDE, 4, 2 * DEPTH, QUART), bf16),
            pltpu.VMEM((4, 2 * ROWS, QUART), f32),
            pltpu.VMEM((2, 4, ROWS, QUART), bf16),
            pltpu.VMEM((layers, depth, wide), bf16),
            pltpu.VMEM((REPLICAS, layers, depth, COLS), bf16),
            pltpu.VMEM((layers, depth, COLS), f32),
            pltpu.VMEM((layers, depth, COLS), f32),
            pltpu.VMEM((layers, depth, COLS), bf16),
            pltpu.VMEM((2, 2), f32),
            pltpu.VMEM((REPLICAS, layers, depth, COLS), bf16),
            pltpu.VMEM((4, 4, 8, 128), f32),
            dma((4, AHEAD + 2)),
            dma((4, REUSE + 2)),
            dma((4,)),
            dma((4,)),
            dma((4,)),
            dma((4,)),
            dma((4,)),
            dma((4,)),
            dma((3,)),
            dma((3,)),
            dma((3,)),
            dma((3,)),
            dma((3,)),
            dma((4, 3)),
            dma((4,)),
            dma((4,)),
            dma((4,)),
            dma((9,)),
            pltpu.SemaphoreType.REGULAR,
        ],
        compiler_params=pltpu.CompilerParams(
            collective_id=0, has_side_effects=True, vmem_limit_bytes=52 * 1024 * 1024
        ),
    )(tokens, next_weights, inner_weights, global_weights, momentum)
    held = [pltpu.with_memory_space_constraint(array, pltpu.VMEM) for array in held]
    return pl.pallas_call(
        write_out,
        name="write_out",
        out_shape=tuple(jax.ShapeDtypeStruct(*result) for result in results),
        in_specs=[any_] * 6,
        out_specs=(any_,) * 6,
        scratch_shapes=[dma((6,))],
        compiler_params=pltpu.CompilerParams(vmem_limit_bytes=8 * 1024 * 1024),
    )(*held)


def solution(mesh):
    placed = (
        P("replica", "fsdp", None),
        P("replica", "fsdp", None),
        P("replica", None, "fsdp", None),
        P(None, "fsdp", "replica"),
        P(None, "fsdp", "replica"),
    )
    return jax.shard_map(
        on_device,
        mesh=mesh,
        in_specs=placed,
        out_specs=(
            P("replica", "fsdp", None),
            P(None, "fsdp", "replica"),
            P(None, "fsdp", "replica"),
            P(None, "fsdp", "replica"),
            P("replica", None, "fsdp", None),
            P(),
        ),
        check_vma=False,
    )
```

```python
import functools

import jax
import jax.numpy as jnp
from jax import lax
from jax.experimental import pallas as pl
from jax.experimental.pallas import tpu as pltpu
from jax.sharding import PartitionSpec as P

MESH = pl.DeviceIdType.MESH
KVW = 1024
SIDE = 4
REPLICAS = 4
DEPTH = 256
QUART = 256
ROWS = 512
COLS = 512
STEPS = 15
AHEAD = 3
REUSE = 2 * AHEAD
CHUNK = 512
outer_rate = 0.7
outer_mom = 0.9
mix_share = 0.5


def build_queues():
    def place(axis, along, across):
        return (along, across) if axis == 0 else (across, along)

    queues = {}
    for axis in (0, 1):
        first = (0, 1) if axis == 0 else (2, 3)
        late = (2, 3) if axis == 0 else (0, 1)
        for sign in (1, -1):
            via, other = (first, late) if sign == 1 else (first[::-1], late[::-1])
            items = [(via[0], 0, 0), (via[1], 0, 0), (other[0], 0, 0), (other[1], 0, 0)]
            items += [(via[0],) + place(axis, -sign, 0)]
            items += [(quarter,) + place(axis, 0, across) for quarter in other for across in (-1, 1)]
            ends = [(quarter,) + place(axis, 0, 2) for quarter in other]
            passed = [(other[0],) + place(axis, -sign, across) for across in (0, -1, 1, 2)]
            items += ends + passed if sign == 1 else ends[:1] + passed + ends[1:]
            queues[axis, sign] = items
    return queues


QUEUES = build_queues()
WAYS = ((0, 1), (0, -1), (1, 1), (1, -1))


def arrivals(step):
    found = []
    for axis, sign in WAYS:
        quarter, ox, oy = QUEUES[axis, sign][step]
        found.append((quarter, ox - sign, oy) if axis == 0 else (quarter, ox, oy - sign))
    return [(quarter, ox % SIDE, oy % SIDE) for quarter, ox, oy in found]


def kernel(
    tokens,
    weights,
    inner,
    outer_in,
    momentum_in,
    projected,
    new_global,
    new_momentum,
    normalized,
    mixed,
    amax_out,
    tok,
    wts,
    acc,
    out_stage,
    inner_v,
    parts,
    outer_v,
    momentum_v,
    normal_v,
    amax_v,
    full,
    peaks,
    ring_send,
    ring_recv,
    tok_here,
    tok_send,
    tok_recv,
    wts_here,
    wts_send,
    wts_recv,
    sum_send,
    sum_recv,
    full_send,
    full_recv,
    peak_send,
    peak_recv,
    out_send,
    out_recv,
    local_sem,
    result_sem,
    greet,
):
    rep = lax.axis_index("replica")
    fsdp = lax.axis_index("fsdp")
    core = fsdp % 2
    x = (fsdp // 2) % SIDE
    y = fsdp // (2 * SIDE)

    def chip_at(ox, oy):
        return ((y + oy + SIDE) % SIDE) * SIDE + (x + ox + SIDE) % SIDE

    def at_plane(ox, oy):
        return {"replica": rep, "fsdp": chip_at(ox, oy) * 2 + core}

    def at_replica(oz):
        return {"replica": (rep + oz + REPLICAS) % REPLICAS, "fsdp": fsdp}

    sibling = {"replica": rep, "fsdp": chip_at(0, 0) * 2 + 1 - core}
    me = chip_at(0, 0)

    def remote(src, dst, send, recv, device):
        return pltpu.make_async_remote_copy(
            src_ref=src, dst_ref=dst, send_sem=send, recv_sem=recv, device_id=device, device_id_type=MESH
        )

    my_rows = pl.ds(pl.multiple_of(core * ROWS, ROWS), ROWS)
    my_depth = pl.ds(pl.multiple_of(core * DEPTH, DEPTH), DEPTH)

    def columns(which, quarter):
        return pl.ds(pl.multiple_of(which * KVW + quarter * QUART, QUART), QUART)

    def start_local(src, dst, sem):
        copy = pltpu.make_async_copy(src, dst, sem)
        copy.start()
        return copy

    def signal(sem, device):
        pl.semaphore_signal(sem, inc=1, device_id=device, device_id_type=MESH)

    axes = ((x, lambda o: at_plane(o, 0)), (y, lambda o: at_plane(0, o)), (rep, at_replica))
    barrier = pltpu.get_barrier_semaphore()
    for place, at in axes:

        @pl.when(place < SIDE - 1)
        def _(at=at):
            signal(barrier, at(1))

        @pl.when(place == 0)
        def _(at=at):
            signal(barrier, at(-1))

    signal(barrier, sibling)
    lower = [jnp.minimum(place, 1) + place // (SIDE - 1) for place, _ in axes]
    pl.semaphore_wait(barrier, 1 + lower[0] + lower[1] + lower[2])
    for axis, (place, at) in enumerate(axes):

        @pl.when(place > 0)
        def _(at=at, axis=axis):
            signal(greet.at[2 * axis], at(-1))

        @pl.when(place == SIDE - 1)
        def _(at=at, axis=axis):
            signal(greet.at[2 * axis + 1], at(1))

    def await_answer(axis, sign):
        place = axes[axis][0]

        @pl.when(place < SIDE - 1 if sign == 1 else place == 0)
        def _():
            pl.semaphore_wait(greet.at[2 * axis + (0 if sign == 1 else 1)], 1)

    def ring_copy(way, step):
        axis, sign = WAYS[way]
        quarter, ox, oy = QUEUES[axis, sign][step]
        device = at_plane(sign, 0) if axis == 0 else at_plane(0, sign)
        block = wts.at[chip_at(ox, oy), quarter]
        if step > 1:
            return [remote(block, block, ring_send.at[way, step % AHEAD], ring_recv.at[way, step % REUSE], device)]
        copies = []
        for half, which in enumerate((core, 1 - core)):
            part = wts.at[me, quarter, pl.ds(pl.multiple_of(which * DEPTH, DEPTH), DEPTH), :]
            src = weights.at[0, :, columns(core, quarter)] if half == 0 else part
            send = ring_send.at[way, step if half == 0 else AHEAD + step]
            recv = ring_recv.at[way, step if half == 0 else REUSE + step]
            copies.append(remote(src, part, send, recv, device))
        return copies

    ring = {(way, step): ring_copy(way, step) for way in range(4) for step in range(AHEAD)}
    w_far = []
    for q in range(4):
        copy = remote(
            weights.at[0, :, columns(1 - core, q)], wts.at[me, q, my_depth, :], wts_send.at[q], wts_recv.at[q], sibling
        )
        copy.start()
        w_far.append(copy)

    def begin(ways):
        for way in ways:
            await_answer(*WAYS[way])
            for step in (0, 1):
                ring[way, step][0].start()

    @pl.when(x == 0)
    def _():
        begin((2, 3, 0, 1))

    @pl.when(x > 0)
    def _():
        begin((0, 1, 2, 3))

    w_here = [
        start_local(weights.at[0, :, columns(core, q)], wts.at[me, q, my_depth, :], wts_here.at[q]) for q in range(4)
    ]

    def sum_copy(oz):
        target = (rep + oz) % REPLICAS
        return remote(
            inner.at[0, :, :, pl.ds(pl.multiple_of(target * COLS, COLS), COLS)],
            parts.at[rep],
            sum_send.at[oz - 1],
            sum_recv.at[oz - 1],
            at_replica(oz),
        )

    sums = [sum_copy(oz) for oz in (1, 2, 3)]
    for copy in w_here:
        copy.wait()
    for copy in w_far:
        copy.wait_recv()
    for step in range(AHEAD):
        for way in range(4):
            ring[way, step][-1].start()

    tok_copies = {}
    for n, oy in enumerate((0, 3, 1, 2)):
        line = (y + oy) % SIDE
        width = SIDE * 2 * DEPTH
        src = tokens.at[0, :, pl.ds(pl.multiple_of(line * width, width), width)]
        dst = tok.at[line, my_rows, :]
        here = start_local(src, dst, tok_here.at[n])
        far = remote(src, dst, tok_send.at[n], tok_recv.at[n], sibling)
        far.start()
        tok_copies[oy] = (here, far)

    own_cols = pl.ds(pl.multiple_of(rep * COLS, COLS), COLS)
    outer_copies = [
        start_local(outer_in, outer_v, local_sem.at[0]),
        start_local(momentum_in, momentum_v, local_sem.at[1]),
        start_local(inner.at[0, :, :, own_cols], parts.at[rep], local_sem.at[2]),
        start_local(inner.at[0], inner_v, local_sem.at[3]),
    ]

    for sign in (1, -1):
        await_answer(2, sign)
    sums[0].start()
    sums[2].start()

    have = set()

    def need_tokens(spots):
        for spot in spots:
            if spot not in have:
                have.add(spot)
                here, far = tok_copies[spot]
                here.wait()
                far.wait_recv()

    def pick(i, values):
        result = values[0]
        for n in range(1, len(values)):
            result = jnp.where(i == n, values[n], result)
        return result

    chunks = 2 * ROWS // CHUNK

    def product(rows, ox, oy, quarter):
        cols = pl.ds(pl.multiple_of(ox * 2 * DEPTH, 2 * DEPTH), 2 * DEPTH)
        return jnp.dot(tok[oy, rows, cols], wts[oy * SIDE + ox, quarter], preferred_element_type=jnp.float32)

    def owner(ox, oy):
        return (x + ox) % SIDE, (y + oy) % SIDE

    def multiply(items, first):
        need_tokens([oy for _, _, oy in items])
        quarters = [q for q, _, _ in items]
        lines = [owner(ox, oy) for _, ox, oy in items]

        def body(i, carry):
            n, m = i // chunks, i % chunks
            quarter = pick(n, quarters)
            ox, oy = pick(n, [line[0] for line in lines]), pick(n, [line[1] for line in lines])
            rows = pl.ds(pl.multiple_of(m * CHUNK, CHUNK), CHUNK)
            part = product(rows, ox, oy, quarter)
            if first:
                acc[quarter, rows, :] = part
            else:
                acc[quarter, rows, :] += part
            return carry

        lax.fori_loop(0, len(items) * chunks, body, 0)

    def out_copy(half, q):
        place = projected.at[0, :, columns(core, q)]
        if half == 0:
            return remote(out_stage.at[0, q], place, out_send.at[q], out_recv.at[q], sibling)
        return pltpu.make_async_copy(out_stage.at[1, q], place, result_sem.at[q])

    def finish(items):
        quarters = list(items)
        lines = [[owner(ox, oy) for ox, oy in items[q]] for q in quarters]

        def body(i, carry):
            half, n = i // len(quarters), i % len(quarters)
            q = pick(n, quarters)
            rows = pl.ds(pl.multiple_of(jnp.where(half == 0, 1 - core, core) * ROWS, ROWS), ROWS)
            value = acc[q, rows, :]
            for spot in range(len(lines[0])):
                ox, oy = (pick(n, [line[spot][axis] for line in lines]) for axis in (0, 1))
                value += product(rows, ox, oy, q)
            out_stage[half, q] = value.astype(jnp.bfloat16)

            @pl.when(half == 0)
            def _():
                out_copy(0, q).start()

            @pl.when(half == 1)
            def _():
                out_copy(1, q).start()

            return carry

        lax.fori_loop(0, 2 * len(quarters), body, 0)

    LINES = 32
    is_value = rep // 2

    results = []

    def update():
        for copy in outer_copies[:3]:
            copy.wait()
        sums[1].wait_recv()
        highest = []
        for layer in range(2):

            def body(i, carry, layer=layer):
                rows = pl.ds(pl.multiple_of(i * LINES, LINES), LINES)
                total = parts[0, layer, rows, :].astype(jnp.float32)
                for r in range(1, REPLICAS):
                    total += parts[r, layer, rows, :].astype(jnp.float32)
                outer = outer_v[layer, rows, :]
                pseudo = outer - total / REPLICAS
                moved = outer_mom * momentum_v[layer, rows, :] + pseudo
                stepped = outer - outer_rate * (pseudo + outer_mom * moved)
                momentum_v[layer, rows, :] = moved
                outer_v[layer, rows, :] = stepped
                full[rep, layer, rows, :] = stepped.astype(jnp.bfloat16)
                return jnp.maximum(carry, jnp.abs(stepped))

            top = lax.fori_loop(0, DEPTH // LINES, body, jnp.zeros((LINES, COLS), jnp.float32))
            highest.append(jnp.max(jnp.max(top, axis=0, keepdims=True), axis=1, keepdims=True))
        results.append(start_local(momentum_v, new_momentum, result_sem.at[4]))
        results.append(start_local(outer_v, new_global, result_sem.at[5]))
        line = lax.broadcasted_iota(jnp.int32, (8, 128), 0)
        tile = jnp.where(
            line == is_value, highest[0], jnp.where(line == 2 + is_value, highest[1], jnp.zeros((8, 128), jnp.float32))
        )
        peak_copies[0] = send_peaks(0, tile)
        copies = []
        for oz in (1, 2, 3):
            copy = remote(
                full.at[rep], full.at[rep], full_send.at[oz - 1], full_recv.at[oz - 1], at_replica(oz)
            )
            copy.start()
            copies.append(copy)
        return copies

    def send_peaks(stage, tile):
        peaks[stage, 0] = tile
        if stage == 3:
            devices = [sibling]
        else:
            devices = [(at_replica(o), at_plane(0, o), at_plane(o, 0))[stage] for o in (1, 2, 3)]
        copies = []
        for n, device in enumerate(devices):
            copy = remote(
                peaks.at[stage, 0], peaks.at[stage, n + 1], peak_send.at[n], peak_recv.at[stage, n], device
            )
            copy.start()
            copies.append(copy)
        return copies

    def take_peaks(stage, copies):
        for copy in copies:
            copy.wait()
        tile = peaks[stage, 0]
        for n in range(len(copies)):
            tile = jnp.maximum(tile, peaks[stage, n + 1])
        return tile

    def normalize(tile):
        values = [[tile[2 * l + t : 2 * l + t + 1, 0:1] for t in range(2)] for l in range(2)]
        row = lax.broadcasted_iota(jnp.int32, (2, 2), 0)
        col = lax.broadcasted_iota(jnp.int32, (2, 2), 1)
        amax_v[...] = jnp.where(
            row == 0,
            jnp.where(col == 0, values[0][0], values[0][1]),
            jnp.where(col == 0, values[1][0], values[1][1]),
        )
        for layer in range(2):
            scale = jnp.where(is_value == 0, values[layer][0], values[layer][1]) + 1e-06

            def body(i, carry, layer=layer, scale=scale):
                rows = pl.ds(pl.multiple_of(i * LINES, LINES), LINES)
                normal_v[layer, rows, :] = (outer_v[layer, rows, :] / scale).astype(jnp.bfloat16)
                return carry

            lax.fori_loop(0, DEPTH // LINES, body, 0)
        results.append(start_local(normal_v, normalized, result_sem.at[6]))
        results.append(start_local(amax_v, amax_out, result_sem.at[7]))

    def mix(copies):
        outer_copies[3].wait()
        for copy in copies:
            copy.wait_recv()

        def body(i, carry):
            layer, n = i // (DEPTH // LINES), i % (DEPTH // LINES)
            rows = pl.ds(pl.multiple_of(n * LINES, LINES), LINES)
            for r in range(REPLICAS):
                cols = slice(r * COLS, (r + 1) * COLS)
                value = mix_share * inner_v[layer, rows, cols].astype(jnp.float32)
                value += (1.0 - mix_share) * full[r, layer, rows, :].astype(jnp.float32)
                inner_v[layer, rows, cols] = value.astype(jnp.bfloat16)
            return carry

        lax.fori_loop(0, 2 * DEPTH // LINES, body, 0)
        results.append(start_local(inner_v, mixed.at[0], result_sem.at[8]))

    multiply([(q, 0, 0) for q in range(4)], True)
    peak_copies = {}
    full_copies = []
    for step in range(STEPS):
        for way in range(4):
            for copy in ring[way, step]:
                copy.wait_recv()
        if step + AHEAD < STEPS:
            for way in range(4):
                for copy in ring[way, step]:
                    copy.wait_send()
                ring[way, step + AHEAD] = ring_copy(way, step + AHEAD)
                ring[way, step + AHEAD][0].start()
        if step < STEPS - 1:
            multiply(arrivals(step), False)
        if step == STEPS - 2:
            finish({1: [], 3: []})
        if step == 2:
            sums[0].wait_recv()
            sums[2].wait_recv()
            sums[1].start()
        if step == 5:
            full_copies = update()
        if step in (7, 9, 11):
            stage = (step - 7) // 2
            tile = take_peaks(stage, peak_copies[stage])
            peak_copies[stage + 1] = send_peaks(stage + 1, tile)
        if step == 12:
            normalize(take_peaks(3, peak_copies[3]))
        if step == 12:
            mix(full_copies)

    last = {}
    for q, ox, oy in arrivals(STEPS - 1):
        last.setdefault(q, []).append((ox, oy))
    need_tokens([oy for items in last.values() for _, oy in items])
    finish(last)

    for way in range(4):
        for step in range(STEPS - AHEAD, STEPS):
            ring[way, step][0].wait_send()
    for copy in w_far + sums + full_copies + [far for _, far in tok_copies.values()]:
        copy.wait_send()
    for copy in [out_copy(half, q) for half in (0, 1) for q in range(4)] + results:
        copy.wait()


def write_out(*refs):
    n = len(refs) // 2
    sem = refs[-1]
    copies = [pltpu.make_async_copy(refs[i], refs[n + i], sem.at[i]) for i in range(n)]
    for copy in copies:
        copy.start()
    for copy in copies:
        copy.wait()


def on_device(tokens, next_weights, inner_weights, global_weights, momentum):
    bf16, f32 = jnp.bfloat16, jnp.float32
    dma = pltpu.SemaphoreType.DMA
    any_ = pl.BlockSpec(memory_space=pl.ANY)
    layers, depth, wide = inner_weights.shape[1:]
    results = (
        ((1, ROWS, 2 * KVW), bf16),
        ((layers, depth, COLS), f32),
        ((layers, depth, COLS), f32),
        ((layers, depth, COLS), bf16),
        ((1, layers, depth, wide), bf16),
        ((2, 2), f32),
    )
    held = pl.pallas_call(
        kernel,
        name="project_and_outer_step",
        out_shape=tuple(pltpu.VMEM(*result) for result in results),
        in_specs=[any_] * 5,
        out_specs=(any_,) * 6,
        scratch_shapes=[
            pltpu.VMEM((SIDE, 2 * ROWS, SIDE * 2 * DEPTH), bf16),
            pltpu.VMEM((SIDE * SIDE, 4, 2 * DEPTH, QUART), bf16),
            pltpu.VMEM((4, 2 * ROWS, QUART), f32),
            pltpu.VMEM((2, 4, ROWS, QUART), bf16),
            pltpu.VMEM((layers, depth, wide), bf16),
            pltpu.VMEM((REPLICAS, layers, depth, COLS), bf16),
            pltpu.VMEM((layers, depth, COLS), f32),
            pltpu.VMEM((layers, depth, COLS), f32),
            pltpu.VMEM((layers, depth, COLS), bf16),
            pltpu.VMEM((2, 2), f32),
            pltpu.VMEM((REPLICAS, layers, depth, COLS), bf16),
            pltpu.VMEM((4, 4, 8, 128), f32),
            dma((4, AHEAD + 2)),
            dma((4, REUSE + 2)),
            dma((4,)),
            dma((4,)),
            dma((4,)),
            dma((4,)),
            dma((4,)),
            dma((4,)),
            dma((3,)),
            dma((3,)),
            dma((3,)),
            dma((3,)),
            dma((3,)),
            dma((4, 3)),
            dma((4,)),
            dma((4,)),
            dma((4,)),
            dma((9,)),
            pltpu.SemaphoreType.REGULAR((6,)),
        ],
        compiler_params=pltpu.CompilerParams(
            collective_id=0, has_side_effects=True, vmem_limit_bytes=52 * 1024 * 1024
        ),
    )(tokens, next_weights, inner_weights, global_weights, momentum)
    held = [pltpu.with_memory_space_constraint(array, pltpu.VMEM) for array in held]
    return pl.pallas_call(
        write_out,
        name="write_out",
        out_shape=tuple(jax.ShapeDtypeStruct(*result) for result in results),
        in_specs=[any_] * 6,
        out_specs=(any_,) * 6,
        scratch_shapes=[dma((6,))],
        compiler_params=pltpu.CompilerParams(vmem_limit_bytes=8 * 1024 * 1024),
    )(*held)


def solution(mesh):
    placed = (
        P("replica", "fsdp", None),
        P("replica", "fsdp", None),
        P("replica", None, "fsdp", None),
        P(None, "fsdp", "replica"),
        P(None, "fsdp", "replica"),
    )
    return jax.shard_map(
        on_device,
        mesh=mesh,
        in_specs=placed,
        out_specs=(
            P("replica", "fsdp", None),
            P(None, "fsdp", "replica"),
            P(None, "fsdp", "replica"),
            P(None, "fsdp", "replica"),
            P("replica", None, "fsdp", None),
            P(),
        ),
        check_vma=False,
    )
```

```python
import functools

import jax
import jax.numpy as jnp
from jax import lax
from jax.experimental import pallas as pl
from jax.experimental.pallas import tpu as pltpu
from jax.sharding import PartitionSpec as P

MESH = pl.DeviceIdType.MESH
KVW = 1024
SIDE = 4
REPLICAS = 4
DEPTH = 256
QUART = 256
ROWS = 512
COLS = 512
STEPS = 15
AHEAD = 2
REUSE = 2 * AHEAD
CHUNK = 512
outer_rate = 0.7
outer_mom = 0.9
mix_share = 0.5


def build_queues():
    def place(axis, along, across):
        return (along, across) if axis == 0 else (across, along)

    queues = {}
    for axis in (0, 1):
        first = (0, 1) if axis == 0 else (2, 3)
        late = (2, 3) if axis == 0 else (0, 1)
        for sign in (1, -1):
            via, other = (first, late) if sign == 1 else (first[::-1], late[::-1])
            items = [(via[0], 0, 0), (via[1], 0, 0), (other[0], 0, 0), (other[1], 0, 0)]
            items += [(via[0],) + place(axis, -sign, 0)]
            items += [(quarter,) + place(axis, 0, across) for quarter in other for across in (-1, 1)]
            ends = [(quarter,) + place(axis, 0, 2) for quarter in other]
            passed = [(other[0],) + place(axis, -sign, across) for across in (0, -1, 1, 2)]
            items += ends + passed if sign == 1 else ends[:1] + passed + ends[1:]
            queues[axis, sign] = items
    return queues


QUEUES = build_queues()
WAYS = ((0, 1), (0, -1), (1, 1), (1, -1))


def arrivals(step):
    found = []
    for axis, sign in WAYS:
        quarter, ox, oy = QUEUES[axis, sign][step]
        found.append((quarter, ox - sign, oy) if axis == 0 else (quarter, ox, oy - sign))
    return [(quarter, ox % SIDE, oy % SIDE) for quarter, ox, oy in found]


def kernel(
    tokens,
    weights,
    inner,
    outer_in,
    momentum_in,
    projected,
    new_global,
    new_momentum,
    normalized,
    mixed,
    amax_out,
    tok,
    wts,
    acc,
    out_stage,
    inner_v,
    parts,
    outer_v,
    momentum_v,
    normal_v,
    amax_v,
    full,
    peaks,
    ring_send,
    ring_recv,
    tok_here,
    tok_send,
    tok_recv,
    sum_send,
    sum_recv,
    full_recv,
    peak_send,
    peak_recv,
    out_send,
    out_recv,
    result_sem,
    greet,
):
    rep = lax.axis_index("replica")
    fsdp = lax.axis_index("fsdp")
    core = fsdp % 2
    x = (fsdp // 2) % SIDE
    y = fsdp // (2 * SIDE)

    def chip_at(ox, oy):
        return ((y + oy + SIDE) % SIDE) * SIDE + (x + ox + SIDE) % SIDE

    def at_plane(ox, oy):
        return {"replica": rep, "fsdp": chip_at(ox, oy) * 2 + core}

    def at_replica(oz):
        return {"replica": (rep + oz + REPLICAS) % REPLICAS, "fsdp": fsdp}

    sibling = {"replica": rep, "fsdp": chip_at(0, 0) * 2 + 1 - core}
    me = chip_at(0, 0)

    def remote(src, dst, send, recv, device):
        return pltpu.make_async_remote_copy(
            src_ref=src, dst_ref=dst, send_sem=send, recv_sem=recv, device_id=device, device_id_type=MESH
        )

    my_rows = pl.ds(pl.multiple_of(core * ROWS, ROWS), ROWS)
    my_depth = pl.ds(pl.multiple_of(core * DEPTH, DEPTH), DEPTH)

    def columns(which, quarter):
        return pl.ds(pl.multiple_of(which * KVW + quarter * QUART, QUART), QUART)

    def start_local(src, dst, sem):
        copy = pltpu.make_async_copy(src, dst, sem)
        copy.start()
        return copy

    def signal(sem, device):
        pl.semaphore_signal(sem, inc=1, device_id=device, device_id_type=MESH)

    axes = ((x, lambda o: at_plane(o, 0)), (y, lambda o: at_plane(0, o)), (rep, at_replica))
    barrier = pltpu.get_barrier_semaphore()
    for place, at in axes:

        @pl.when(place < SIDE - 1)
        def _(at=at):
            signal(barrier, at(1))

        @pl.when(place == 0)
        def _(at=at):
            signal(barrier, at(-1))

    signal(barrier, sibling)
    lower = [jnp.minimum(place, 1) + place // (SIDE - 1) for place, _ in axes]
    pl.semaphore_wait(barrier, 1 + lower[0] + lower[1] + lower[2])
    for axis, (place, at) in enumerate(axes):

        @pl.when(place > 0)
        def _(at=at, axis=axis):
            signal(greet.at[2 * axis], at(-1))

        @pl.when(place == SIDE - 1)
        def _(at=at, axis=axis):
            signal(greet.at[2 * axis + 1], at(1))

    def await_answer(axis, sign):
        place = axes[axis][0]

        @pl.when(place < SIDE - 1 if sign == 1 else place == 0)
        def _():
            pl.semaphore_wait(greet.at[2 * axis + (0 if sign == 1 else 1)], 1)

    def ring_copy(way, step):
        axis, sign = WAYS[way]
        quarter, ox, oy = QUEUES[axis, sign][step]
        device = at_plane(sign, 0) if axis == 0 else at_plane(0, sign)
        block = wts.at[chip_at(ox, oy), quarter]
        if step > 1:
            return [remote(block, block, ring_send.at[way, step % AHEAD], ring_recv.at[way, step % REUSE], device)]
        copies = []
        for half, which in enumerate((core, 1 - core)):
            part = wts.at[me, quarter, pl.ds(pl.multiple_of(which * DEPTH, DEPTH), DEPTH), :]
            src = weights.at[0, :, columns(core, quarter)] if half == 0 else part
            send = ring_send.at[way, step if half == 0 else AHEAD + step]
            recv = ring_recv.at[way, step if half == 0 else REUSE + step]
            copies.append(remote(src, part, send, recv, device))
        return copies

    ring = {(way, step): ring_copy(way, step) for way in range(4) for step in range(AHEAD)}
    w_far = []
    for q in range(4):
        copy = remote(
            weights.at[0, :, columns(1 - core, q)], wts.at[me, q, my_depth, :], out_send.at[q], out_recv.at[q], sibling
        )
        copy.start()
        w_far.append(copy)

    def begin(ways):
        for way in ways:
            await_answer(*WAYS[way])
            for step in (0, 1):
                ring[way, step][0].start()

    @pl.when(x == 0)
    def _():
        begin((2, 3, 0, 1))

    @pl.when(x > 0)
    def _():
        begin((0, 1, 2, 3))

    w_here = [
        start_local(weights.at[0, :, columns(core, q)], wts.at[me, q, my_depth, :], result_sem.at[q]) for q in range(4)
    ]

    def sum_copy(oz):
        target = (rep + oz) % REPLICAS
        return remote(
            inner.at[0, :, :, pl.ds(pl.multiple_of(target * COLS, COLS), COLS)],
            parts.at[rep],
            sum_send.at[oz - 1],
            sum_recv.at[oz - 1],
            at_replica(oz),
        )

    sums = [sum_copy(oz) for oz in (1, 2, 3)]
    for copy in w_here:
        copy.wait()
    for copy in w_far:
        copy.wait_recv()
    for step in range(AHEAD):
        for way in range(4):
            ring[way, step][-1].start()

    tok_copies = {}
    for n, oy in enumerate((0, 3, 1, 2)):
        line = (y + oy) % SIDE
        width = SIDE * 2 * DEPTH
        src = tokens.at[0, :, pl.ds(pl.multiple_of(line * width, width), width)]
        dst = tok.at[line, my_rows, :]
        here = start_local(src, dst, tok_here.at[n])
        far = remote(src, dst, tok_send.at[n], tok_recv.at[n], sibling)
        far.start()
        tok_copies[oy] = (here, far)

    own_cols = pl.ds(pl.multiple_of(rep * COLS, COLS), COLS)
    outer_copies = [
        start_local(outer_in, outer_v, result_sem.at[4]),
        start_local(momentum_in, momentum_v, result_sem.at[5]),
        start_local(inner.at[0, :, :, own_cols], parts.at[rep], result_sem.at[6]),
        start_local(inner.at[0], inner_v, result_sem.at[8]),
    ]

    for sign in (1, -1):
        await_answer(2, sign)
    sums[0].start()
    sums[2].start()

    have = set()

    def need_tokens(spots):
        for spot in spots:
            if spot not in have:
                have.add(spot)
                here, far = tok_copies[spot]
                here.wait()
                far.wait_recv()

    def pick(i, values):
        result = values[0]
        for n in range(1, len(values)):
            result = jnp.where(i == n, values[n], result)
        return result

    chunks = 2 * ROWS // CHUNK

    def product(rows, ox, oy, quarter):
        cols = pl.ds(pl.multiple_of(ox * 2 * DEPTH, 2 * DEPTH), 2 * DEPTH)
        return jnp.dot(tok[oy, rows, cols], wts[oy * SIDE + ox, quarter], preferred_element_type=jnp.float32)

    def owner(ox, oy):
        return (x + ox) % SIDE, (y + oy) % SIDE

    def multiply(items, first):
        need_tokens([oy for _, _, oy in items])
        quarters = [q for q, _, _ in items]
        lines = [owner(ox, oy) for _, ox, oy in items]

        def body(i, carry):
            n, m = i // chunks, i % chunks
            quarter = pick(n, quarters)
            ox, oy = pick(n, [line[0] for line in lines]), pick(n, [line[1] for line in lines])
            rows = pl.ds(pl.multiple_of(m * CHUNK, CHUNK), CHUNK)
            part = product(rows, ox, oy, quarter)
            if first:
                acc[quarter, rows, :] = part
            else:
                acc[quarter, rows, :] += part
            return carry

        lax.fori_loop(0, len(items) * chunks, body, 0)

    def out_copy(half, q):
        place = projected.at[0, :, columns(core, q)]
        if half == 0:
            return remote(out_stage.at[0, q], place, out_send.at[q], out_recv.at[q], sibling)
        return pltpu.make_async_copy(out_stage.at[1, q], place, result_sem.at[q])

    def finish(items):
        quarters = list(items)
        lines = [[owner(ox, oy) for ox, oy in items[q]] for q in quarters]

        def body(i, carry):
            half, n = i // len(quarters), i % len(quarters)
            q = pick(n, quarters)
            rows = pl.ds(pl.multiple_of(jnp.where(half == 0, 1 - core, core) * ROWS, ROWS), ROWS)
            value = acc[q, rows, :]
            for spot in range(len(lines[0])):
                ox, oy = (pick(n, [line[spot][axis] for line in lines]) for axis in (0, 1))
                value += product(rows, ox, oy, q)
            out_stage[half, q] = value.astype(jnp.bfloat16)

            @pl.when(half == 0)
            def _():
                out_copy(0, q).start()

            @pl.when(half == 1)
            def _():
                out_copy(1, q).start()

            return carry

        lax.fori_loop(0, 2 * len(quarters), body, 0)

    LINES = 32
    is_value = rep // 2

    results = []

    def update():
        for copy in outer_copies[:3]:
            copy.wait()
        sums[1].wait_recv()
        for copy in sums:
            copy.wait_send()
        highest = []
        for layer in range(2):

            def body(i, carry, layer=layer):
                rows = pl.ds(pl.multiple_of(i * LINES, LINES), LINES)
                total = parts[0, layer, rows, :].astype(jnp.float32)
                for r in range(1, REPLICAS):
                    total += parts[r, layer, rows, :].astype(jnp.float32)
                outer = outer_v[layer, rows, :]
                pseudo = outer - total / REPLICAS
                moved = outer_mom * momentum_v[layer, rows, :] + pseudo
                stepped = outer - outer_rate * (pseudo + outer_mom * moved)
                momentum_v[layer, rows, :] = moved
                outer_v[layer, rows, :] = stepped
                full[rep, layer, rows, :] = stepped.astype(jnp.bfloat16)
                return jnp.maximum(carry, jnp.abs(stepped))

            top = lax.fori_loop(0, DEPTH // LINES, body, jnp.zeros((LINES, COLS), jnp.float32))
            highest.append(jnp.max(jnp.max(top, axis=0, keepdims=True), axis=1, keepdims=True))
        results.append(start_local(momentum_v, new_momentum, result_sem.at[4]))
        results.append(start_local(outer_v, new_global, result_sem.at[5]))
        line = lax.broadcasted_iota(jnp.int32, (8, 128), 0)
        tile = jnp.where(
            line == is_value, highest[0], jnp.where(line == 2 + is_value, highest[1], jnp.zeros((8, 128), jnp.float32))
        )
        peak_copies[0] = send_peaks(0, tile)
        copies = []
        for oz in (1, 2, 3):
            copy = remote(
                full.at[rep], full.at[rep], sum_send.at[oz - 1], full_recv.at[oz - 1], at_replica(oz)
            )
            copy.start()
            copies.append(copy)
        return copies

    def send_peaks(stage, tile):
        peaks[stage, 0] = tile
        if stage == 3:
            devices = [sibling]
        else:
            devices = [(at_replica(o), at_plane(0, o), at_plane(o, 0))[stage] for o in (1, 2, 3)]
        copies = []
        for n, device in enumerate(devices):
            copy = remote(
                peaks.at[stage, 0], peaks.at[stage, n + 1], peak_send.at[n], peak_recv.at[stage, n], device
            )
            copy.start()
            copies.append(copy)
        return copies

    def take_peaks(stage, copies):
        for copy in copies:
            copy.wait()
        tile = peaks[stage, 0]
        for n in range(len(copies)):
            tile = jnp.maximum(tile, peaks[stage, n + 1])
        return tile

    def normalize(tile):
        values = [[tile[2 * l + t : 2 * l + t + 1, 0:1] for t in range(2)] for l in range(2)]
        row = lax.broadcasted_iota(jnp.int32, (2, 2), 0)
        col = lax.broadcasted_iota(jnp.int32, (2, 2), 1)
        amax_v[...] = jnp.where(
            row == 0,
            jnp.where(col == 0, values[0][0], values[0][1]),
            jnp.where(col == 0, values[1][0], values[1][1]),
        )
        for layer in range(2):
            scale = jnp.where(is_value == 0, values[layer][0], values[layer][1]) + 1e-06

            def body(i, carry, layer=layer, scale=scale):
                rows = pl.ds(pl.multiple_of(i * LINES, LINES), LINES)
                normal_v[layer, rows, :] = (outer_v[layer, rows, :] / scale).astype(jnp.bfloat16)
                return carry

            lax.fori_loop(0, DEPTH // LINES, body, 0)
        results.append(start_local(normal_v, normalized, result_sem.at[6]))
        results.append(start_local(amax_v, amax_out, result_sem.at[7]))

    def mix(copies):
        outer_copies[3].wait()
        for copy in copies:
            copy.wait_recv()

        def body(i, carry):
            layer, n = i // (DEPTH // LINES), i % (DEPTH // LINES)
            rows = pl.ds(pl.multiple_of(n * LINES, LINES), LINES)
            for r in range(REPLICAS):
                cols = slice(r * COLS, (r + 1) * COLS)
                value = mix_share * inner_v[layer, rows, cols].astype(jnp.float32)
                value += (1.0 - mix_share) * full[r, layer, rows, :].astype(jnp.float32)
                inner_v[layer, rows, cols] = value.astype(jnp.bfloat16)
            return carry

        lax.fori_loop(0, 2 * DEPTH // LINES, body, 0)
        results.append(start_local(inner_v, mixed.at[0], result_sem.at[8]))

    multiply([(q, 0, 0) for q in range(4)], True)
    peak_copies = {}
    full_copies = []
    for step in range(STEPS - 1):
        for way in range(4):
            for copy in ring[way, step]:
                copy.wait_recv()
        if step + AHEAD < STEPS:
            for way in range(4):
                for copy in ring[way, step]:
                    copy.wait_send()
                ring[way, step + AHEAD] = ring_copy(way, step + AHEAD)
                ring[way, step + AHEAD][0].start()
        multiply(arrivals(step), False)
        if step == STEPS - 2:
            finish({1: [], 3: []})
        if step == 2:
            sums[0].wait_recv()
            sums[2].wait_recv()
            sums[1].start()
            for copy in w_far:
                copy.wait_send()
        if step == 5:
            full_copies = update()
        if step in (7, 9, 11):
            stage = (step - 7) // 2
            tile = take_peaks(stage, peak_copies[stage])
            peak_copies[stage + 1] = send_peaks(stage + 1, tile)
        if step == 12:
            normalize(take_peaks(3, peak_copies[3]))
        if step == 12:
            mix(full_copies)

    last = {}
    for q, ox, oy in arrivals(STEPS - 1):
        last.setdefault(q, []).append((ox, oy))
    need_tokens([oy for items in last.values() for _, oy in items])

    def conclude(ways):
        for pair in ways:
            for way in pair:
                ring[way, STEPS - 1][0].wait_recv()
            q = arrivals(STEPS - 1)[pair[0]][0]
            finish({q: last[q]})

    @pl.when(x == 0)
    def _():
        conclude(((2, 3), (0, 1)))

    @pl.when(x > 0)
    def _():
        conclude(((0, 1), (2, 3)))

    for way in range(4):
        for step in range(STEPS - AHEAD, STEPS):
            ring[way, step][0].wait_send()
    for copy in full_copies + [far for _, far in tok_copies.values()]:
        copy.wait_send()
    for copy in [out_copy(half, q) for half in (0, 1) for q in range(4)] + results:
        copy.wait()


def write_out(*refs):
    n = len(refs) // 2
    sem = refs[-1]
    copies = [pltpu.make_async_copy(refs[i], refs[n + i], sem.at[i]) for i in range(n)]
    for copy in copies:
        copy.start()
    for copy in copies:
        copy.wait()


def on_device(tokens, next_weights, inner_weights, global_weights, momentum):
    bf16, f32 = jnp.bfloat16, jnp.float32
    dma = pltpu.SemaphoreType.DMA
    any_ = pl.BlockSpec(memory_space=pl.ANY)
    layers, depth, wide = inner_weights.shape[1:]
    results = (
        ((1, ROWS, 2 * KVW), bf16),
        ((layers, depth, COLS), f32),
        ((layers, depth, COLS), f32),
        ((layers, depth, COLS), bf16),
        ((1, layers, depth, wide), bf16),
        ((2, 2), f32),
    )
    held = pl.pallas_call(
        kernel,
        name="project_and_outer_step",
        out_shape=tuple(pltpu.VMEM(*result) for result in results),
        in_specs=[any_] * 5,
        out_specs=(any_,) * 6,
        scratch_shapes=[
            pltpu.VMEM((SIDE, 2 * ROWS, SIDE * 2 * DEPTH), bf16),
            pltpu.VMEM((SIDE * SIDE, 4, 2 * DEPTH, QUART), bf16),
            pltpu.VMEM((4, 2 * ROWS, QUART), f32),
            pltpu.VMEM((2, 4, ROWS, QUART), bf16),
            pltpu.VMEM((layers, depth, wide), bf16),
            pltpu.VMEM((REPLICAS, layers, depth, COLS), bf16),
            pltpu.VMEM((layers, depth, COLS), f32),
            pltpu.VMEM((layers, depth, COLS), f32),
            pltpu.VMEM((layers, depth, COLS), bf16),
            pltpu.VMEM((2, 2), f32),
            pltpu.VMEM((REPLICAS, layers, depth, COLS), bf16),
            pltpu.VMEM((4, 4, 8, 128), f32),
            dma((4, AHEAD + 2)),
            dma((4, REUSE + 2)),
            dma((4,)),
            dma((4,)),
            dma((4,)),
            dma((3,)),
            dma((3,)),
            dma((3,)),
            dma((3,)),
            dma((4, 3)),
            dma((4,)),
            dma((4,)),
            dma((9,)),
            pltpu.SemaphoreType.REGULAR((6,)),
        ],
        compiler_params=pltpu.CompilerParams(
            collective_id=0, has_side_effects=True, vmem_limit_bytes=52 * 1024 * 1024
        ),
    )(tokens, next_weights, inner_weights, global_weights, momentum)
    held = [pltpu.with_memory_space_constraint(array, pltpu.VMEM) for array in held]
    return pl.pallas_call(
        write_out,
        name="write_out",
        out_shape=tuple(jax.ShapeDtypeStruct(*result) for result in results),
        in_specs=[any_] * 6,
        out_specs=(any_,) * 6,
        scratch_shapes=[dma((6,))],
        compiler_params=pltpu.CompilerParams(vmem_limit_bytes=8 * 1024 * 1024),
    )(*held)


def solution(mesh):
    placed = (
        P("replica", "fsdp", None),
        P("replica", "fsdp", None),
        P("replica", None, "fsdp", None),
        P(None, "fsdp", "replica"),
        P(None, "fsdp", "replica"),
    )
    return jax.shard_map(
        on_device,
        mesh=mesh,
        in_specs=placed,
        out_specs=(
            P("replica", "fsdp", None),
            P(None, "fsdp", "replica"),
            P(None, "fsdp", "replica"),
            P(None, "fsdp", "replica"),
            P("replica", None, "fsdp", None),
            P(),
        ),
        check_vma=False,
    )
```

```python
import functools

import jax
import jax.numpy as jnp
from jax import lax
from jax.experimental import pallas as pl
from jax.experimental.pallas import tpu as pltpu
from jax.sharding import PartitionSpec as P

MESH = pl.DeviceIdType.MESH
KVW = 1024
SIDE = 4
REPLICAS = 4
DEPTH = 256
QUART = 256
ROWS = 512
COLS = 512
STEPS = 15
AHEAD = 2
REUSE = 2 * AHEAD
CHUNK = 1024
outer_rate = 0.7
outer_mom = 0.9
mix_share = 0.5


def build_queues():
    def place(axis, along, across):
        return (along, across) if axis == 0 else (across, along)

    queues = {}
    for axis in (0, 1):
        first = (0, 1) if axis == 0 else (2, 3)
        late = (2, 3) if axis == 0 else (0, 1)
        for sign in (1, -1):
            via, other = (first, late) if sign == 1 else (first[::-1], late[::-1])
            items = [(via[0], 0, 0), (via[1], 0, 0), (other[0], 0, 0), (other[1], 0, 0)]
            items += [(via[0],) + place(axis, -sign, 0)]
            items += [(quarter,) + place(axis, 0, across) for quarter in other for across in (-1, 1)]
            ends = [(quarter,) + place(axis, 0, 2) for quarter in other]
            passed = [(other[0],) + place(axis, -sign, across) for across in (0, -1, 1, 2)]
            items += ends + passed if sign == 1 else ends[:1] + passed + ends[1:]
            queues[axis, sign] = items
    return queues


QUEUES = build_queues()
WAYS = ((0, 1), (0, -1), (1, 1), (1, -1))


def arrivals(step):
    found = []
    for axis, sign in WAYS:
        quarter, ox, oy = QUEUES[axis, sign][step]
        found.append((quarter, ox - sign, oy) if axis == 0 else (quarter, ox, oy - sign))
    return [(quarter, ox % SIDE, oy % SIDE) for quarter, ox, oy in found]


def kernel(
    tokens,
    weights,
    inner,
    outer_in,
    momentum_in,
    projected,
    new_global,
    new_momentum,
    normalized,
    mixed,
    amax_out,
    tok,
    wts,
    acc,
    out_stage,
    inner_v,
    parts,
    outer_v,
    momentum_v,
    normal_v,
    amax_v,
    full,
    peaks,
    ring_send,
    ring_recv,
    tok_here,
    tok_send,
    tok_recv,
    sum_send,
    sum_recv,
    full_recv,
    peak_send,
    peak_recv,
    out_send,
    out_recv,
    result_sem,
    greet,
):
    rep = lax.axis_index("replica")
    fsdp = lax.axis_index("fsdp")
    core = fsdp % 2
    x = (fsdp // 2) % SIDE
    y = fsdp // (2 * SIDE)

    def chip_at(ox, oy):
        return ((y + oy + SIDE) % SIDE) * SIDE + (x + ox + SIDE) % SIDE

    def at_plane(ox, oy):
        return {"replica": rep, "fsdp": chip_at(ox, oy) * 2 + core}

    def at_replica(oz):
        return {"replica": (rep + oz + REPLICAS) % REPLICAS, "fsdp": fsdp}

    sibling = {"replica": rep, "fsdp": chip_at(0, 0) * 2 + 1 - core}
    me = chip_at(0, 0)

    def remote(src, dst, send, recv, device):
        return pltpu.make_async_remote_copy(
            src_ref=src, dst_ref=dst, send_sem=send, recv_sem=recv, device_id=device, device_id_type=MESH
        )

    my_rows = pl.ds(pl.multiple_of(core * ROWS, ROWS), ROWS)
    my_depth = pl.ds(pl.multiple_of(core * DEPTH, DEPTH), DEPTH)

    def columns(which, quarter):
        return pl.ds(pl.multiple_of(which * KVW + quarter * QUART, QUART), QUART)

    def start_local(src, dst, sem):
        copy = pltpu.make_async_copy(src, dst, sem)
        copy.start()
        return copy

    def signal(sem, device):
        pl.semaphore_signal(sem, inc=1, device_id=device, device_id_type=MESH)

    axes = ((x, lambda o: at_plane(o, 0)), (y, lambda o: at_plane(0, o)), (rep, at_replica))
    barrier = pltpu.get_barrier_semaphore()
    for place, at in axes:

        @pl.when(place < SIDE - 1)
        def _(at=at):
            signal(barrier, at(1))

        @pl.when(place == 0)
        def _(at=at):
            signal(barrier, at(-1))

    signal(barrier, sibling)
    lower = [jnp.minimum(place, 1) + place // (SIDE - 1) for place, _ in axes]
    pl.semaphore_wait(barrier, 1 + lower[0] + lower[1] + lower[2])
    for axis, (place, at) in enumerate(axes):

        @pl.when(place > 0)
        def _(at=at, axis=axis):
            signal(greet.at[2 * axis], at(-1))

        @pl.when(place == SIDE - 1)
        def _(at=at, axis=axis):
            signal(greet.at[2 * axis + 1], at(1))

    def await_answer(axis, sign):
        place = axes[axis][0]

        @pl.when(place < SIDE - 1 if sign == 1 else place == 0)
        def _():
            pl.semaphore_wait(greet.at[2 * axis + (0 if sign == 1 else 1)], 1)

    def ring_copy(way, step):
        axis, sign = WAYS[way]
        quarter, ox, oy = QUEUES[axis, sign][step]
        device = at_plane(sign, 0) if axis == 0 else at_plane(0, sign)
        block = wts.at[chip_at(ox, oy), quarter]
        if step > 1:
            return [remote(block, block, ring_send.at[way, step % AHEAD], ring_recv.at[way, step % REUSE], device)]
        copies = []
        for half, which in enumerate((core, 1 - core)):
            part = wts.at[me, quarter, pl.ds(pl.multiple_of(which * DEPTH, DEPTH), DEPTH), :]
            src = weights.at[0, :, columns(core, quarter)] if half == 0 else part
            send = ring_send.at[way, step if half == 0 else AHEAD + step]
            recv = ring_recv.at[way, step if half == 0 else REUSE + step]
            copies.append(remote(src, part, send, recv, device))
        return copies

    ring = {(way, step): ring_copy(way, step) for way in range(4) for step in range(AHEAD)}
    w_far = []
    for q in range(4):
        copy = remote(
            weights.at[0, :, columns(1 - core, q)], wts.at[me, q, my_depth, :], out_send.at[q], out_recv.at[q], sibling
        )
        copy.start()
        w_far.append(copy)

    def begin(ways):
        for way in ways:
            await_answer(*WAYS[way])
            for step in (0, 1):
                ring[way, step][0].start()

    @pl.when(x == 0)
    def _():
        begin((2, 3, 0, 1))

    @pl.when(x > 0)
    def _():
        begin((0, 1, 2, 3))

    w_here = [
        start_local(weights.at[0, :, columns(core, q)], wts.at[me, q, my_depth, :], result_sem.at[q]) for q in range(4)
    ]

    def sum_copy(oz):
        target = (rep + oz) % REPLICAS
        return remote(
            inner.at[0, :, :, pl.ds(pl.multiple_of(target * COLS, COLS), COLS)],
            parts.at[rep],
            sum_send.at[oz - 1],
            sum_recv.at[oz - 1],
            at_replica(oz),
        )

    sums = [sum_copy(oz) for oz in (1, 2, 3)]
    for copy in w_here:
        copy.wait()
    for copy in w_far:
        copy.wait_recv()
    for step in range(AHEAD):
        for way in range(4):
            ring[way, step][-1].start()

    tok_copies = {}
    for n, oy in enumerate((0, 3, 1, 2)):
        line = (y + oy) % SIDE
        width = SIDE * 2 * DEPTH
        src = tokens.at[0, :, pl.ds(pl.multiple_of(line * width, width), width)]
        dst = tok.at[line, my_rows, :]
        here = start_local(src, dst, tok_here.at[n])
        far = remote(src, dst, tok_send.at[n], tok_recv.at[n], sibling)
        far.start()
        tok_copies[oy] = (here, far)

    own_cols = pl.ds(pl.multiple_of(rep * COLS, COLS), COLS)
    outer_copies = [
        start_local(outer_in, outer_v, result_sem.at[4]),
        start_local(momentum_in, momentum_v, result_sem.at[5]),
        start_local(inner.at[0, :, :, own_cols], parts.at[rep], result_sem.at[6]),
        start_local(inner.at[0], inner_v, result_sem.at[8]),
    ]

    for sign in (1, -1):
        await_answer(2, sign)
    sums[0].start()
    sums[2].start()

    have = set()

    def need_tokens(spots):
        for spot in spots:
            if spot not in have:
                have.add(spot)
                here, far = tok_copies[spot]
                here.wait()
                far.wait_recv()

    def pick(i, values):
        result = values[0]
        for n in range(1, len(values)):
            result = jnp.where(i == n, values[n], result)
        return result

    chunks = 2 * ROWS // CHUNK

    def product(rows, ox, oy, quarter):
        cols = pl.ds(pl.multiple_of(ox * 2 * DEPTH, 2 * DEPTH), 2 * DEPTH)
        return jnp.dot(tok[oy, rows, cols], wts[oy * SIDE + ox, quarter], preferred_element_type=jnp.float32)

    def owner(ox, oy):
        return (x + ox) % SIDE, (y + oy) % SIDE

    def multiply(items, first):
        need_tokens([oy for _, _, oy in items])
        quarters = [q for q, _, _ in items]
        lines = [owner(ox, oy) for _, ox, oy in items]

        def body(i, carry):
            n, m = i // chunks, i % chunks
            quarter = pick(n, quarters)
            ox, oy = pick(n, [line[0] for line in lines]), pick(n, [line[1] for line in lines])
            rows = pl.ds(pl.multiple_of(m * CHUNK, CHUNK), CHUNK)
            part = product(rows, ox, oy, quarter)
            if first:
                acc[quarter, rows, :] = part
            else:
                acc[quarter, rows, :] += part
            return carry

        lax.fori_loop(0, len(items) * chunks, body, 0)

    def out_copy(half, q):
        place = projected.at[0, :, columns(core, q)]
        if half == 0:
            return remote(out_stage.at[0, q], place, out_send.at[q], out_recv.at[q], sibling)
        return pltpu.make_async_copy(out_stage.at[1, q], place, result_sem.at[q])

    def finish(items):
        quarters = list(items)
        lines = [[owner(ox, oy) for ox, oy in items[q]] for q in quarters]

        def body(i, carry):
            half, n = i // len(quarters), i % len(quarters)
            q = pick(n, quarters)
            rows = pl.ds(pl.multiple_of(jnp.where(half == 0, 1 - core, core) * ROWS, ROWS), ROWS)
            value = acc[q, rows, :]
            for spot in range(len(lines[0])):
                ox, oy = (pick(n, [line[spot][axis] for line in lines]) for axis in (0, 1))
                value += product(rows, ox, oy, q)
            out_stage[half, q] = value.astype(jnp.bfloat16)

            @pl.when(half == 0)
            def _():
                out_copy(0, q).start()

            @pl.when(half == 1)
            def _():
                out_copy(1, q).start()

            return carry

        lax.fori_loop(0, 2 * len(quarters), body, 0)

    LINES = 32
    is_value = rep // 2

    results = []

    def update():
        for copy in outer_copies[:3]:
            copy.wait()
        sums[1].wait_recv()
        for copy in sums:
            copy.wait_send()
        highest = []
        for layer in range(2):

            def body(i, carry, layer=layer):
                rows = pl.ds(pl.multiple_of(i * LINES, LINES), LINES)
                total = parts[0, layer, rows, :].astype(jnp.float32)
                for r in range(1, REPLICAS):
                    total += parts[r, layer, rows, :].astype(jnp.float32)
                outer = outer_v[layer, rows, :]
                pseudo = outer - total / REPLICAS
                moved = outer_mom * momentum_v[layer, rows, :] + pseudo
                stepped = outer - outer_rate * (pseudo + outer_mom * moved)
                momentum_v[layer, rows, :] = moved
                outer_v[layer, rows, :] = stepped
                full[rep, layer, rows, :] = stepped.astype(jnp.bfloat16)
                return jnp.maximum(carry, jnp.abs(stepped))

            top = lax.fori_loop(0, DEPTH // LINES, body, jnp.zeros((LINES, COLS), jnp.float32))
            highest.append(jnp.max(jnp.max(top, axis=0, keepdims=True), axis=1, keepdims=True))
        results.append(start_local(momentum_v, new_momentum, result_sem.at[4]))
        results.append(start_local(outer_v, new_global, result_sem.at[5]))
        line = lax.broadcasted_iota(jnp.int32, (8, 128), 0)
        tile = jnp.where(
            line == is_value, highest[0], jnp.where(line == 2 + is_value, highest[1], jnp.zeros((8, 128), jnp.float32))
        )
        peak_copies[0] = send_peaks(0, tile)
        copies = []
        for oz in (1, 2, 3):
            copy = remote(
                full.at[rep], full.at[rep], sum_send.at[oz - 1], full_recv.at[oz - 1], at_replica(oz)
            )
            copy.start()
            copies.append(copy)
        return copies

    def send_peaks(stage, tile):
        peaks[stage, 0] = tile
        if stage == 3:
            devices = [sibling]
        else:
            devices = [(at_replica(o), at_plane(0, o), at_plane(o, 0))[stage] for o in (1, 2, 3)]
        copies = []
        for n, device in enumerate(devices):
            copy = remote(
                peaks.at[stage, 0], peaks.at[stage, n + 1], peak_send.at[n], peak_recv.at[stage, n], device
            )
            copy.start()
            copies.append(copy)
        return copies

    def take_peaks(stage, copies):
        for copy in copies:
            copy.wait()
        tile = peaks[stage, 0]
        for n in range(len(copies)):
            tile = jnp.maximum(tile, peaks[stage, n + 1])
        return tile

    def normalize(tile):
        values = [[tile[2 * l + t : 2 * l + t + 1, 0:1] for t in range(2)] for l in range(2)]
        row = lax.broadcasted_iota(jnp.int32, (2, 2), 0)
        col = lax.broadcasted_iota(jnp.int32, (2, 2), 1)
        amax_v[...] = jnp.where(
            row == 0,
            jnp.where(col == 0, values[0][0], values[0][1]),
            jnp.where(col == 0, values[1][0], values[1][1]),
        )
        for layer in range(2):
            scale = jnp.where(is_value == 0, values[layer][0], values[layer][1]) + 1e-06

            def body(i, carry, layer=layer, scale=scale):
                rows = pl.ds(pl.multiple_of(i * LINES, LINES), LINES)
                normal_v[layer, rows, :] = (outer_v[layer, rows, :] / scale).astype(jnp.bfloat16)
                return carry

            lax.fori_loop(0, DEPTH // LINES, body, 0)
        results.append(start_local(normal_v, normalized, result_sem.at[6]))
        results.append(start_local(amax_v, amax_out, result_sem.at[7]))

    def mix(copies):
        outer_copies[3].wait()
        for copy in copies:
            copy.wait_recv()

        def body(i, carry):
            layer, n = i // (DEPTH // LINES), i % (DEPTH // LINES)
            rows = pl.ds(pl.multiple_of(n * LINES, LINES), LINES)
            for r in range(REPLICAS):
                cols = slice(r * COLS, (r + 1) * COLS)
                value = mix_share * inner_v[layer, rows, cols].astype(jnp.float32)
                value += (1.0 - mix_share) * full[r, layer, rows, :].astype(jnp.float32)
                inner_v[layer, rows, cols] = value.astype(jnp.bfloat16)
            return carry

        lax.fori_loop(0, 2 * DEPTH // LINES, body, 0)
        results.append(start_local(inner_v, mixed.at[0], result_sem.at[8]))

    multiply([(q, 0, 0) for q in range(4)], True)
    peak_copies = {}
    full_copies = []
    for step in range(STEPS - 1):
        for way in range(4):
            for copy in ring[way, step]:
                copy.wait_recv()
        if step + AHEAD < STEPS:
            for way in range(4):
                for copy in ring[way, step]:
                    copy.wait_send()
                ring[way, step + AHEAD] = ring_copy(way, step + AHEAD)
                ring[way, step + AHEAD][0].start()
        multiply(arrivals(step), False)
        if step == STEPS - 2:
            finish({1: [], 3: []})
        if step == 2:
            sums[0].wait_recv()
            sums[2].wait_recv()
            sums[1].start()
            for copy in w_far:
                copy.wait_send()
        if step == 5:
            full_copies = update()
        if step in (7, 9, 11):
            stage = (step - 7) // 2
            tile = take_peaks(stage, peak_copies[stage])
            peak_copies[stage + 1] = send_peaks(stage + 1, tile)
        if step == 12:
            normalize(take_peaks(3, peak_copies[3]))
        if step == 12:
            mix(full_copies)

    last = {}
    for q, ox, oy in arrivals(STEPS - 1):
        last.setdefault(q, []).append((ox, oy))
    need_tokens([oy for items in last.values() for _, oy in items])

    def conclude(ways):
        for pair in ways:
            for way in pair:
                ring[way, STEPS - 1][0].wait_recv()
            q = arrivals(STEPS - 1)[pair[0]][0]
            finish({q: last[q]})

    @pl.when(x == 0)
    def _():
        conclude(((2, 3), (0, 1)))

    @pl.when(x > 0)
    def _():
        conclude(((0, 1), (2, 3)))

    for way in range(4):
        for step in range(STEPS - AHEAD, STEPS):
            ring[way, step][0].wait_send()
    for copy in full_copies + [far for _, far in tok_copies.values()]:
        copy.wait_send()
    for copy in [out_copy(half, q) for half in (0, 1) for q in range(4)] + results:
        copy.wait()


def write_out(*refs):
    n = len(refs) // 2
    sem = refs[-1]
    copies = [pltpu.make_async_copy(refs[i], refs[n + i], sem.at[i]) for i in range(n)]
    for copy in copies:
        copy.start()
    for copy in copies:
        copy.wait()


def on_device(tokens, next_weights, inner_weights, global_weights, momentum):
    bf16, f32 = jnp.bfloat16, jnp.float32
    dma = pltpu.SemaphoreType.DMA
    any_ = pl.BlockSpec(memory_space=pl.ANY)
    layers, depth, wide = inner_weights.shape[1:]
    results = (
        ((1, ROWS, 2 * KVW), bf16),
        ((layers, depth, COLS), f32),
        ((layers, depth, COLS), f32),
        ((layers, depth, COLS), bf16),
        ((1, layers, depth, wide), bf16),
        ((2, 2), f32),
    )
    held = pl.pallas_call(
        kernel,
        name="project_and_outer_step",
        out_shape=tuple(pltpu.VMEM(*result) for result in results),
        in_specs=[any_] * 5,
        out_specs=(any_,) * 6,
        scratch_shapes=[
            pltpu.VMEM((SIDE, 2 * ROWS, SIDE * 2 * DEPTH), bf16),
            pltpu.VMEM((SIDE * SIDE, 4, 2 * DEPTH, QUART), bf16),
            pltpu.VMEM((4, 2 * ROWS, QUART), f32),
            pltpu.VMEM((2, 4, ROWS, QUART), bf16),
            pltpu.VMEM((layers, depth, wide), bf16),
            pltpu.VMEM((REPLICAS, layers, depth, COLS), bf16),
            pltpu.VMEM((layers, depth, COLS), f32),
            pltpu.VMEM((layers, depth, COLS), f32),
            pltpu.VMEM((layers, depth, COLS), bf16),
            pltpu.VMEM((2, 2), f32),
            pltpu.VMEM((REPLICAS, layers, depth, COLS), bf16),
            pltpu.VMEM((4, 4, 8, 128), f32),
            dma((4, AHEAD + 2)),
            dma((4, REUSE + 2)),
            dma((4,)),
            dma((4,)),
            dma((4,)),
            dma((3,)),
            dma((3,)),
            dma((3,)),
            dma((3,)),
            dma((4, 3)),
            dma((4,)),
            dma((4,)),
            dma((9,)),
            pltpu.SemaphoreType.REGULAR((6,)),
        ],
        compiler_params=pltpu.CompilerParams(
            collective_id=0, has_side_effects=True, vmem_limit_bytes=52 * 1024 * 1024
        ),
    )(tokens, next_weights, inner_weights, global_weights, momentum)
    held = [pltpu.with_memory_space_constraint(array, pltpu.VMEM) for array in held]
    return pl.pallas_call(
        write_out,
        name="write_out",
        out_shape=tuple(jax.ShapeDtypeStruct(*result) for result in results),
        in_specs=[any_] * 6,
        out_specs=(any_,) * 6,
        scratch_shapes=[dma((6,))],
        compiler_params=pltpu.CompilerParams(vmem_limit_bytes=8 * 1024 * 1024),
    )(*held)


def solution(mesh):
    placed = (
        P("replica", "fsdp", None),
        P("replica", "fsdp", None),
        P("replica", None, "fsdp", None),
        P(None, "fsdp", "replica"),
        P(None, "fsdp", "replica"),
    )
    return jax.shard_map(
        on_device,
        mesh=mesh,
        in_specs=placed,
        out_specs=(
            P("replica", "fsdp", None),
            P(None, "fsdp", "replica"),
            P(None, "fsdp", "replica"),
            P(None, "fsdp", "replica"),
            P("replica", None, "fsdp", None),
            P(),
        ),
        check_vma=False,
    )
```
